1024 devices in a mesh: grp: 64 (over z, core), rep: 16 (over y, x).
Axes of the slice: x: 4, y: 4, z: 32, core: 2. Of those that a mesh axis runs over, the one named last changes fastest.
Arguments:
- user_factors: float32 [131072, 256], P(('grp', 'rep'))
- item_factors: float32 [524288, 256], P(('grp', 'rep')), may hold values from -3 to 3
- tile_users: int32 [65536], P(('grp', 'rep')), may hold values from 0 to 2047, as said below
- tile_counts: int32 [65536, 64, 128], P(('grp', 'rep')), may hold values from 0 to 5
Outputs:
- item_solution: float32 [524288, 256], P(('grp', 'rep'))
The draws below stay inside these ranges and needn't reach their ends.
Inputs may be any that keep to these rules, and one draw needn't show every extreme that they name: `tile_users`: users and items are laid out in 64 x 16 equal shards in the order of the mesh (grp slowest). Every tile names a row block of the shard with the same rep index as its own shard, and all tiles of one shard that name blocks of one user shard name the same block. The first tile of every shard names a block of the shard whose grp index is 32 away, counted round.
All inputs are finite; a program needn't handle non-finite values.
Results may differ from the reference program's by a relative error of at most 0.0026.
Values may be sent and summed in bfloat16 or wider, within the bound.
No kernel may reach another device: no remote copies, remote signals or barrier semaphores. Data moves between devices by JAX's collectives and lax.ppermute only.
A program may use at most 32 MiB of HBM per device.

```python
import math
import jax
import jax.numpy as jnp
from jax import lax

K = 256
UROWS = 64
IBLK = 128
ITERS = 3
IB_DEV = 4
TPB = 16
UB_DEV = 2
TILES_DEV = 64
TILES = 65536
USER_BLOCKS = 2048
USERS = 131072
ITEMS = 524288
N_GRP = 64
N_REP = 16


def draw_user_factors(key, part):
    key = jax.random.fold_in(key, 5)
    first_key, second_key = jax.random.split(key, 2)
    columns = jnp.exp(jax.random.uniform(first_key, (K,), jnp.float32, math.log(0.3), math.log(3.0)))
    overall = 4.0 / math.sqrt(USERS)
    values = jax.random.normal(second_key, (USERS, K), jnp.float32)
    return (values * columns[None, :] * overall).astype(jnp.float32)


def draw_tile_users(key, part):
    key = jax.random.fold_in(key, 17)
    first_key, second_key, third_key = jax.random.split(key, 3)
    devices = N_GRP * N_REP
    half = N_GRP // 2
    device_ids = jnp.arange(devices, dtype=jnp.int32)
    member = device_ids // N_REP
    replica = device_ids % N_REP
    chosen = jax.random.randint(first_key, (devices, N_GRP), 0, UB_DEV, dtype=jnp.int32)
    low_device = half * N_REP
    high_device = (half - 1) % N_GRP * N_REP + N_REP - 1
    chosen = chosen.at[low_device, 0].set(0).at[high_device, N_GRP - 1].set(UB_DEV - 1)
    spread = jax.random.randint(second_key, (devices, 1), max(N_GRP // 4, 1), N_GRP + 1, dtype=jnp.int32)
    offset = jax.random.randint(third_key, (devices, TILES_DEV), 0, 1 << 20, dtype=jnp.int32) % spread
    holder = (member[:, None] + offset - spread // 2) % N_GRP
    holder = holder.at[:, 0].set((member + half) % N_GRP)
    within = jnp.take_along_axis(chosen, holder, axis=1)
    block_ids = (holder * N_REP + replica[:, None]) * UB_DEV + within
    return block_ids.reshape(-1).astype(jnp.int32)


def touch_ends(values, key, least, high):
    extent = values.shape
    index_at = [jax.random.randint(jax.random.fold_in(key, axis), (), 0, extent[axis]) for axis in range(len(extent))]
    values = values.at[tuple(index_at)].set(least)
    longest = extent.index(max(extent))
    index_at[longest] = (index_at[longest] + 1) % extent[longest]
    return values.at[tuple(index_at)].set(high)


def steps_of(own_key, dims, cuts, smallest, top_value):
    level = 1.0
    for dim, blocks in cuts:
        heights = jax.random.uniform(jax.random.fold_in(jax.random.fold_in(own_key, 6), dim), (blocks,), jnp.float32, smallest / len(cuts), top_value / len(cuts))
        level = level * jnp.repeat(jnp.exp(heights), dims[dim] // blocks).reshape((-1,) + (1,) * (len(dims) - 1 - dim))
    return level


def gaussian(rng, dims, width, reach, cuts=(), kind=jnp.bfloat16):
    drawn = jax.random.normal(rng, dims, jnp.float32) * width
    if len(cuts) > 0:
        drawn = steps_of(rng, dims, cuts, -0.22, 0.18) * drawn
    return jnp.clip(drawn, min=-reach, max=reach).astype(kind)


def setup_inputs(seed: int = 0) -> dict:
    key_list = jax.random.split(jax.random.key(seed), 5)
    user_factors = draw_user_factors(jax.random.fold_in(key_list[4], 71), 0)
    item_factors = gaussian(key_list[1], (ITEMS, K), 0.5, 3.0, ((0, 1024),), jnp.float32)
    tile_users = draw_tile_users(jax.random.fold_in(key_list[4], 71), 0)
    tile_counts = touch_ends(jax.random.randint(key_list[3], (TILES, UROWS, IBLK), 0, 6), jax.random.fold_in(key_list[3], 1), 0, 5).astype(jnp.int32)
    return {"user_factors": user_factors, "item_factors": item_factors, "tile_users": tile_users, "tile_counts": tile_counts}


ALPHA = 8.0
LAMBDA = 1.0
EPSILON = 1e-6


def conjugate(initial, target, operate):
    solution = initial
    residue = target - operate(solution)
    direction = residue
    current = jnp.sum(residue * residue, axis=1, keepdims=True)
    for iteration in range(ITERS):
        applied = operate(direction)
        step_size = current / (jnp.sum(direction * applied, axis=1, keepdims=True) + EPSILON)
        solution = solution + step_size * direction
        residue = residue - step_size * applied
        following = jnp.sum(residue * residue, axis=1, keepdims=True)
        direction = residue + (following / (current + EPSILON)) * direction
        current = following
    return solution


def reference(user_factors, item_factors, tile_users, tile_counts):
    highest = lax.Precision.HIGHEST
    gramian = jnp.dot(user_factors.T, user_factors, precision=highest, preferred_element_type=jnp.float32)
    user_blocks = user_factors.astype(jnp.bfloat16).reshape(USER_BLOCKS, UROWS, K)

    def one_device(device):
        tile_ids = lax.dynamic_slice_in_dim(tile_users, device * TILES_DEV, TILES_DEV)
        tile_rows = user_blocks[tile_ids].astype(jnp.float32).reshape(IB_DEV, TPB, UROWS, K)
        counts = lax.dynamic_slice_in_dim(tile_counts, device * TILES_DEV, TILES_DEV)
        counts = counts.astype(jnp.float32).reshape(IB_DEV, TPB, UROWS, IBLK)
        initial = lax.dynamic_slice_in_dim(item_factors, device * (IB_DEV * IBLK), IB_DEV * IBLK)
        confidence = jnp.where(counts > 0, 1.0 + ALPHA * counts, 0.0).astype(jnp.bfloat16)
        confidence = lax.optimization_barrier(confidence).astype(jnp.float32)
        target = jnp.einsum("bsui,bsuk->bik", confidence, tile_rows, precision=highest).reshape(-1, K)

        def operate(direction):
            rounded = lax.optimization_barrier(direction.astype(jnp.bfloat16)).astype(jnp.float32)
            rounded = rounded.reshape(IB_DEV, IBLK, K)
            scores = jnp.einsum("bsuk,bik->bsui", tile_rows, rounded, precision=highest)
            mixed_terms = (ALPHA * counts * scores).astype(jnp.bfloat16)
            mixed_terms = lax.optimization_barrier(mixed_terms).astype(jnp.float32)
            tile_part = jnp.einsum("bsui,bsuk->bik", mixed_terms, tile_rows, precision=highest).reshape(-1, K)
            return jnp.dot(direction, gramian, precision=highest, preferred_element_type=jnp.float32) + LAMBDA * direction + tile_part

        return conjugate(initial, target, operate)

    solved = lax.map(one_device, jnp.arange(N_GRP * N_REP, dtype=jnp.int32))
    return solved.reshape(ITEMS, K)
```

```python
import functools

import jax
import jax.numpy as jnp
import numpy as np
from jax import lax
from jax.experimental import pallas as pl
from jax.experimental.pallas import tpu as pltpu
from jax.sharding import PartitionSpec as P

UROWS = 64
IBLK = 128
ITERS = 3
CORES = 2
STRIDE = 8
CHUNK = 256

ALPHA = 8.0
LAMBDA = 1.0
EPSILON = 1e-06


def chip_shift(value, chips, distance):
    pairs = [
        (CORES * chip + core, CORES * ((chip + distance) % chips) + core)
        for chip in range(chips)
        for core in range(CORES)
    ]
    return lax.ppermute(value, "grp", pairs)


def core_swap(value, chips):
    pairs = [(CORES * chip + core, CORES * chip + 1 - core) for chip in range(chips) for core in range(CORES)]
    return lax.ppermute(value, "grp", pairs)


def slot_table(chips):
    pack_slot = {0: 0, chips - STRIDE: 1, STRIDE: 2, 2 * STRIDE: 3}
    table = np.full((chips,), -1, np.int32)
    for pack, offset in enumerate([0, -1, -2, -3, 1, 2, 3]):
        for ahead, slot in pack_slot.items():
            table[(offset + ahead) % chips] = 4 * pack + slot
    for slot, ahead in enumerate([-4 - STRIDE, -4 + STRIDE, 4 - STRIDE, 4 + STRIDE]):
        table[ahead % chips] = 28 + slot
    assert (table >= 0).all()
    return table


def gram_kernel(users_ref, gram_ref):
    users = users_ref[...]
    high = users.astype(jnp.bfloat16)
    low = (users - high.astype(jnp.float32)).astype(jnp.bfloat16)
    dims = (((0,), (0,)), ((), ()))
    product = functools.partial(lax.dot_general, dimension_numbers=dims, preferred_element_type=jnp.float32)
    gram_ref[...] = product(high, high) + (product(high, low) + product(low, high))


def local_gram(users):
    features = users.shape[1]
    return pl.pallas_call(
        gram_kernel,
        out_shape=jax.ShapeDtypeStruct((features, features), jnp.float32),
        in_specs=[pl.BlockSpec(memory_space=pltpu.VMEM)],
        out_specs=pl.BlockSpec(memory_space=pltpu.VMEM),
    )(users)


def solve_kernel(
    tiles_ref, slots_ref, place_ref, near_ref, other_ref, near_last_ref, other_last_ref, counts_ref, items_ref,
    gram_ref, out_ref, rows_ref, turned_ref, weight_ref, high_ref, low_ref, guess_ref, residue_ref, direction_ref,
    applied_ref,
):
    tile_total = counts_ref.shape[0]
    features, items = guess_ref.shape
    blocks = items // IBLK
    depth = rows_ref.shape[0] // blocks
    chips = slots_ref.shape[0]
    replicas, owned = place_ref[2], place_ref[3]
    near_blocks = near_ref.shape[0] // UROWS

    def fetch(tile, carry):
        block = tiles_ref[tile]
        within = lax.rem(block, owned)
        member = lax.div(lax.div(block, owned), replicas)
        chip, core = lax.div(member, CORES), lax.rem(member, CORES)
        ahead = lax.rem(chip - place_ref[0] + chips, chips)
        place = slots_ref[ahead] * owned + within
        last = place >= near_blocks
        mine = core == place_ref[1]
        to = pl.ds(pl.multiple_of(tile * UROWS, UROWS), UROWS)
        at = pl.ds(pl.multiple_of(place * UROWS, UROWS), UROWS)
        at_last = pl.ds(pl.multiple_of((place - near_blocks) * UROWS, UROWS), UROWS)

        @pl.when(mine & ~last)
        def _():
            rows_ref[to, :] = near_ref[at, :]

        @pl.when(~mine & ~last)
        def _():
            rows_ref[to, :] = other_ref[at, :]

        @pl.when(mine & last)
        def _():
            rows_ref[to, :] = near_last_ref[at_last, :]

        @pl.when(~mine & last)
        def _():
            rows_ref[to, :] = other_last_ref[at_last, :]

        return carry

    lax.fori_loop(0, tile_total, fetch, 0)

    gram = gram_ref[...]
    gram_high = gram.astype(jnp.bfloat16)
    high_ref[...] = gram_high
    low_ref[...] = (gram - gram_high.astype(jnp.float32)).astype(jnp.bfloat16)

    def dot(left, right):
        return jnp.dot(left, right, preferred_element_type=jnp.float32)

    def columns(block):
        return slice(block * IBLK, (block + 1) * IBLK)

    def operate(vector, block):
        high = vector.astype(jnp.bfloat16)
        low = (vector - high.astype(jnp.float32)).astype(jnp.bfloat16)
        total = vector * LAMBDA + dot(high_ref[...], high) + (dot(low_ref[...], high) + dot(high_ref[...], low))
        for start in range(0, depth, CHUNK):
            span = slice(block * depth + start, block * depth + start + CHUNK)
            scores = dot(rows_ref[span, :], high)
            mixed = (weight_ref[span, :] * scores).astype(jnp.bfloat16)
            total = total + dot(turned_ref[block, :, start : start + CHUNK], mixed)
        return total

    per_block = tile_total // blocks
    squares = []
    for block in range(blocks):
        turned_ref[block] = rows_ref[block * depth : (block + 1) * depth, :].T
        target = jnp.zeros((features, IBLK), jnp.float32)
        for start in range(0, depth, CHUNK):
            span = slice(block * depth + start, block * depth + start + CHUNK)
            first = block * per_block + start // UROWS
            counts = counts_ref[first : first + CHUNK // UROWS].reshape(CHUNK, IBLK).astype(jnp.float32)
            weight = ALPHA * counts
            weight_ref[span, :] = weight
            confidence = jnp.where(counts > 0, 1.0 + weight, 0.0).astype(jnp.bfloat16)
            target = target + dot(turned_ref[block, :, start : start + CHUNK], confidence)
        guess = items_ref[columns(block), :].T
        guess_ref[:, columns(block)] = guess
        residue = target - operate(guess, block)
        residue_ref[:, columns(block)] = residue
        direction_ref[:, columns(block)] = residue
        squares.append(jnp.sum(residue * residue, axis=0, keepdims=True))

    def step(iteration, squares):
        nexts = []
        for block in range(blocks):
            applied_ref[:, columns(block)] = operate(direction_ref[:, columns(block)], block)
        for block in range(blocks):
            current = squares[block]
            direction = direction_ref[:, columns(block)]
            applied = applied_ref[:, columns(block)]
            size = current / (jnp.sum(direction * applied, axis=0, keepdims=True) + EPSILON)
            guess_ref[:, columns(block)] += size * direction
            residue = residue_ref[:, columns(block)] - size * applied
            residue_ref[:, columns(block)] = residue
            following = jnp.sum(residue * residue, axis=0, keepdims=True)
            direction_ref[:, columns(block)] = residue + (following / (current + EPSILON)) * direction
            nexts.append(following)
        return tuple(nexts)

    lax.fori_loop(0, ITERS, step, tuple(squares))
    for block in range(blocks):
        out_ref[columns(block), :] = guess_ref[:, columns(block)].T


def solve(tile_users, slots, place, near, other, near_last, other_last, counts, items, gram):
    item_total, features = items.shape
    tile_total = counts.shape[0]
    depth = tile_total * UROWS
    blocks = item_total // IBLK
    state = pltpu.VMEM((features, item_total), jnp.float32)
    scalar, vector = pl.BlockSpec(memory_space=pltpu.SMEM), pl.BlockSpec(memory_space=pltpu.VMEM)
    return pl.pallas_call(
        solve_kernel,
        out_shape=jax.ShapeDtypeStruct(items.shape, jnp.float32),
        in_specs=[scalar] * 3 + [vector] * 7,
        out_specs=vector,
        scratch_shapes=[
            pltpu.VMEM((depth, features), jnp.bfloat16),
            pltpu.VMEM((blocks, features, depth // blocks), jnp.bfloat16),
            pltpu.VMEM((depth, IBLK), jnp.float32),
            pltpu.VMEM((features, features), jnp.bfloat16),
            pltpu.VMEM((features, features), jnp.bfloat16),
            state,
            state,
            state,
            state,
        ],
        compiler_params=pltpu.CompilerParams(vmem_limit_bytes=40 * 1024 * 1024),
    )(tile_users, slots, place, near, other, near_last, other_last, counts, items, gram)


def on_device(user_factors, item_factors, tile_users, tile_counts):
    chips = lax.axis_size("grp") // CORES
    replicas = lax.axis_size("rep")
    owned_rows, features = user_factors.shape
    share = features // replicas
    half = owned_rows // 2
    shift = functools.partial(chip_shift, chips=chips)
    bar = lax.optimization_barrier

    own = user_factors.astype(jnp.bfloat16)
    below, above = shift(own, distance=STRIDE), shift(own, distance=-STRIDE)
    pieces = lax.all_to_all(local_gram(user_factors), "rep", 0, 0, tiled=True)
    gram = jnp.sum(pieces.reshape(replicas, share, features), axis=0)
    below, above, gram = bar((below, above, gram))

    far_first, far_last = shift(below[:half], distance=STRIDE), shift(above[half:], distance=-STRIDE)
    gram = gram + core_swap(gram, chips)
    gram = gram + shift(gram, distance=STRIDE)
    far_first, far_last, gram = bar((far_first, far_last, gram))

    pack = jnp.concatenate([own, below, above, far_first, far_last])
    ups, downs = [pack], [pack]
    for hop in range(3):
        up, down = shift(ups[-1], distance=1), shift(downs[-1], distance=-1)
        if hop == 0:
            gram = gram + shift(gram, distance=2 * STRIDE)
        elif hop == 1:
            gram = gram + shift(gram, distance=1) + (shift(gram, distance=2) + shift(gram, distance=3))
        else:
            gram = gram + shift(gram, distance=4)
        up, down, gram = bar((up, down, gram))
        ups.append(up)
        downs.append(down)

    middle = slice(owned_rows, 3 * owned_rows)
    up, down = shift(ups[-1][middle], distance=1), shift(downs[-1][middle], distance=-1)
    near = jnp.concatenate(ups + downs[1:])
    other = core_swap(near, chips)
    gram = lax.all_to_all(jnp.concatenate([gram] * replicas), "rep", 0, 0, tiled=True)
    up, down, other, gram = bar((up, down, other, gram))
    near_last = jnp.concatenate([up, down])
    other_last = core_swap(near_last, chips)

    member = lax.axis_index("grp")
    place = jnp.stack([member // CORES, member % CORES, replicas, owned_rows // UROWS]).astype(jnp.int32)
    slots = jnp.asarray(slot_table(chips))
    return solve(
        tile_users, slots, place, near, other, near_last, other_last, tile_counts, item_factors, gram
    )


def solution(mesh):
    in_specs = (
        P(("grp", "rep"), None),
        P(("grp", "rep"), None),
        P(("grp", "rep")),
        P(("grp", "rep"), None, None),
    )
    out_specs = P(("grp", "rep"), None)
    return jax.shard_map(
        on_device, mesh=mesh, in_specs=in_specs, out_specs=out_specs, check_vma=False
    )
```

```python
import functools

import jax
import jax.numpy as jnp
import numpy as np
from jax import lax
from jax.experimental import pallas as pl
from jax.experimental.pallas import tpu as pltpu
from jax.sharding import PartitionSpec as P

UROWS = 64
IBLK = 128
ITERS = 3
CORES = 2
STRIDE = 8
CHUNK = 256
PACK = 4
HOPS = 3

ALPHA = 8.0
LAMBDA = 1.0
EPSILON = 1e-06


def chip_shift(value, chips, distance):
    pairs = [
        (CORES * chip + core, CORES * ((chip + distance) % chips) + core)
        for chip in range(chips)
        for core in range(CORES)
    ]
    return lax.ppermute(value, "grp", pairs)


def core_swap(value, chips):
    pairs = [(CORES * chip + core, CORES * chip + 1 - core) for chip in range(chips) for core in range(CORES)]
    return lax.ppermute(value, "grp", pairs)


def slot_table(chips):
    pack_slot = {0: 0, 2 * STRIDE: 1, chips - STRIDE: 2, STRIDE: 3}
    table = np.full((chips,), -1, np.int32)
    for pack, offset in enumerate([0, -1, 1, -2, 2, -3, 3]):
        for ahead, slot in pack_slot.items():
            table[(offset + ahead) % chips] = PACK * pack + slot
    for slot, ahead in enumerate([-4 - STRIDE, -4 + STRIDE, 4 - STRIDE, 4 + STRIDE]):
        table[ahead % chips] = PACK * (2 * HOPS + 1) + slot
    assert (table >= 0).all()
    return table


def pool_places(tile_users, chips, replicas, owned):
    member = tile_users // (owned * replicas)
    here = lax.axis_index("grp")
    ahead = (member // CORES - here // CORES + chips) % chips
    distances = np.arange(chips, dtype=np.int32)
    slot = jnp.sum(jnp.where(ahead[:, None] == distances, slot_table(chips), 0), axis=1)
    other_core = (member % CORES != here % CORES).astype(jnp.int32)
    return ((other_core * chips + slot) * owned + tile_users % owned).astype(jnp.int32)


def merge(parts):
    half = parts.shape[0] // 2
    return parts[:half].astype(jnp.float32) + parts[half:].astype(jnp.float32)


def dot(left, right):
    return jnp.dot(left, right, preferred_element_type=jnp.float32)


def dot_turned(left, right):
    return lax.dot_general(left, right, (((1,), (1,)), ((), ())), preferred_element_type=jnp.float32)


def high_low(value):
    high = value.astype(jnp.bfloat16)
    return high, (value - high.astype(jnp.float32)).astype(jnp.bfloat16)


def item_rows(block):
    return slice(block * IBLK, (block + 1) * IBLK)


SCALAR = pl.BlockSpec(memory_space=pltpu.SMEM)
VECTOR = pl.BlockSpec(memory_space=pltpu.VMEM)
PARAMS = pltpu.CompilerParams(vmem_limit_bytes=40 * 1024 * 1024)


def gram_kernel(users_ref, gram_ref):
    high, low = high_low(users_ref[...])
    dims = (((0,), (0,)), ((), ()))
    product = functools.partial(lax.dot_general, dimension_numbers=dims, preferred_element_type=jnp.float32)
    gram_ref[...] = product(high, high) + (product(high, low) + product(low, high))


def local_gram(users):
    features = users.shape[1]
    return pl.pallas_call(
        gram_kernel,
        out_shape=jax.ShapeDtypeStruct((features, features), jnp.float32),
        in_specs=[VECTOR],
        out_specs=VECTOR,
        cost_estimate=pl.CostEstimate(flops=10**10, bytes_accessed=10**7, transcendentals=0),
        name="local_gram",
    )(users)


def weight_kernel(counts_ref, weight_ref):
    blocks, _, depth = weight_ref.shape
    tiles = IBLK // UROWS
    for block in range(blocks):
        for start in range(0, depth, IBLK):
            first = (block * depth + start) // UROWS
            counts = counts_ref[first : first + tiles].reshape(IBLK, IBLK).astype(jnp.float32)
            weight_ref[block, :, start : start + IBLK] = (ALPHA * counts).T.astype(jnp.bfloat16)


def item_weights(counts, blocks):
    depth = counts.shape[0] * counts.shape[1] // blocks
    return pl.pallas_call(
        weight_kernel,
        out_shape=jax.ShapeDtypeStruct((blocks, IBLK, depth), jnp.bfloat16),
        in_specs=[VECTOR],
        out_specs=VECTOR,
        compiler_params=PARAMS,
        name="item_weights",
    )(counts)


def tile_part(total, high, block, rows_ref, weight_ref):
    depth = weight_ref.shape[2]
    for start in range(0, depth, CHUNK):
        rows = rows_ref[block * depth + start : block * depth + start + CHUNK, :]
        scores = dot_turned(high, rows)
        weight = weight_ref[block, :, start : start + CHUNK].astype(jnp.float32)
        total = total + dot((weight * scores).astype(jnp.bfloat16), rows)
    return total


def first_kernel(places_ref, *refs):
    gathered, (weight_ref, items_ref, rows_ref, residue_ref, pool_ref) = refs[:-5], refs[-5:]
    filled = 0
    for part in gathered:
        pool_ref[filled : filled + part.shape[0], :] = part[...]
        filled += part.shape[0]

    def fetch(tile, carry):
        to = pl.ds(pl.multiple_of(tile * UROWS, UROWS), UROWS)
        at = pl.ds(pl.multiple_of(places_ref[tile] * UROWS, UROWS), UROWS)
        rows_ref[to, :] = pool_ref[at, :]
        return carry

    lax.fori_loop(0, places_ref.shape[0], fetch, 0, unroll=4)
    blocks, _, depth = weight_ref.shape
    for block in range(blocks):
        guess = items_ref[item_rows(block), :]
        target = -LAMBDA * guess
        for start in range(0, depth, CHUNK):
            weight = weight_ref[block, :, start : start + CHUNK]
            confidence = weight + jnp.where(weight > 0, 1.0, 0.0).astype(jnp.bfloat16)
            target = target + dot(confidence, rows_ref[block * depth + start : block * depth + start + CHUNK, :])
        part = tile_part(jnp.zeros_like(guess), guess.astype(jnp.bfloat16), block, rows_ref, weight_ref)
        residue_ref[item_rows(block), :] = target - part


def first_residue(places, gathered, weight, items):
    blocks, _, depth = weight.shape
    features = items.shape[1]
    pool_rows = sum(part.shape[0] for part in gathered)
    return pl.pallas_call(
        first_kernel,
        out_shape=(
            jax.ShapeDtypeStruct((blocks * depth, features), jnp.bfloat16),
            jax.ShapeDtypeStruct(items.shape, jnp.float32),
        ),
        in_specs=[SCALAR] + [VECTOR] * (len(gathered) + 2),
        out_specs=(VECTOR, VECTOR),
        scratch_shapes=[pltpu.VMEM((pool_rows, features), jnp.bfloat16)],
        compiler_params=PARAMS,
        name="first_residue",
    )(places, *gathered, weight, items)


def steps_kernel(
    rows_ref, weight_ref, items_ref, started_ref, gram_ref, guess_ref, high_ref, low_ref, residue_ref, direction_ref,
    applied_ref,
):
    blocks = weight_ref.shape[0]
    high_ref[...], low_ref[...] = high_low(gram_ref[...])

    def gram_part(vector):
        high, low = high_low(vector)
        return dot(high, high_ref[...]) + (dot(high, low_ref[...]) + dot(low, high_ref[...]))

    guess = items_ref[...]
    guess_ref[...] = guess
    residue = started_ref[...] - gram_part(guess)
    residue_ref[...] = residue
    direction_ref[...] = residue

    def step(iteration, current):
        vector = direction_ref[...]
        applied_ref[...] = vector * LAMBDA + gram_part(vector)
        for block in range(blocks):
            span = item_rows(block)
            high = direction_ref[span, :].astype(jnp.bfloat16)
            applied_ref[span, :] = tile_part(applied_ref[span, :], high, block, rows_ref, weight_ref)
        direction = direction_ref[...]
        applied = applied_ref[...]
        size = current / (jnp.sum(direction * applied, axis=1, keepdims=True) + EPSILON)
        guess_ref[...] += size * direction
        residue = residue_ref[...] - size * applied
        residue_ref[...] = residue
        following = jnp.sum(residue * residue, axis=1, keepdims=True)
        direction_ref[...] = residue + (following / (current + EPSILON)) * direction
        return following

    lax.fori_loop(0, ITERS, step, jnp.sum(residue * residue, axis=1, keepdims=True))


def solve_steps(rows, weight, items, started, gram):
    features = items.shape[1]
    state = pltpu.VMEM(items.shape, jnp.float32)
    square = pltpu.VMEM((features, features), jnp.bfloat16)
    return pl.pallas_call(
        steps_kernel,
        out_shape=jax.ShapeDtypeStruct(items.shape, jnp.float32),
        in_specs=[VECTOR] * 5,
        out_specs=VECTOR,
        scratch_shapes=[square, square, state, state, state],
        compiler_params=PARAMS,
        name="solve_steps",
    )(rows, weight, items, started, gram)


def small_call(kernel, outs, name, *args):
    return pl.pallas_call(
        kernel,
        out_shape=outs,
        in_specs=[VECTOR] * len(args),
        out_specs=jax.tree.map(lambda _: VECTOR, outs),
        compiler_params=PARAMS,
        name=name,
    )(*args)


def put_parts(ref, start, value):
    count = value.shape[0]
    ref[start : start + count, :], ref[start + count : start + 2 * count, :] = high_low(value)


def far_kernel(below_ref, above_ref, mine_ref, other_ref, up_ref, down_ref, total_ref):
    half = below_ref.shape[0] // 2
    total = mine_ref[...] + other_ref[...]
    total_ref[...] = total
    up_ref[:half, :] = below_ref[:half, :]
    down_ref[:half, :] = above_ref[half:, :]
    put_parts(up_ref, half, total)
    put_parts(down_ref, half, total)


def pack_kernel(own_ref, below_ref, above_ref, up_ref, down_ref, total_ref, farthest_ref, pack_ref):
    rows = own_ref.shape[0]
    half = rows // 2
    pack_ref[:rows, :] = own_ref[...]
    pack_ref[rows : rows + half, :] = up_ref[:half, :]
    pack_ref[rows + half : 2 * rows, :] = down_ref[:half, :]
    pack_ref[2 * rows : 3 * rows, :] = below_ref[...]
    pack_ref[3 * rows : 4 * rows, :] = above_ref[...]
    total = total_ref[...] + (merge(up_ref[half:, :]) + merge(down_ref[half:, :])) + merge(farthest_ref[...])
    put_parts(pack_ref, PACK * rows, total)


def join_kernel(counts, *refs):
    filled = 0
    for count, part in zip(counts, refs[:-1]):
        refs[-1][filled : filled + count, :] = part[:count, :]
        filled += count


def join(parts, counts):
    out = jax.ShapeDtypeStruct((sum(counts), parts[0].shape[1]), parts[0].dtype)
    return small_call(functools.partial(join_kernel, counts), out, "join", *parts)


def spread_kernel(*refs):
    parts, out_ref = refs[:-1], refs[-1]
    copies, share, _ = out_ref.shape
    total = functools.reduce(jnp.add, [merge(part[-2 * share :, :]) for part in parts])
    for copy in range(copies):
        out_ref[copy] = total


def on_device(user_factors, item_factors, tile_users, tile_counts):
    chips = lax.axis_size("grp") // CORES
    replicas = lax.axis_size("rep")
    owned_rows, features = user_factors.shape
    share = features // replicas
    half = owned_rows // 2
    pack_rows = PACK * owned_rows
    shift = functools.partial(chip_shift, chips=chips)
    bar = lax.optimization_barrier

    def half_rows(count):
        return jax.ShapeDtypeStruct((count, features), jnp.bfloat16)

    piece = jax.ShapeDtypeStruct((share, features), jnp.float32)

    own = user_factors.astype(jnp.bfloat16)
    below, above = shift(own, distance=STRIDE), shift(own, distance=-STRIDE)
    pieces = lax.all_to_all(local_gram(user_factors), "rep", 0, 0, tiled=True)
    gram = jnp.sum(pieces.reshape(replicas, share, features), axis=0)
    gram_other = core_swap(gram, chips)
    below, above, gram, gram_other = bar((below, above, gram, gram_other))

    sent = half_rows(half + 2 * share)
    to_up, to_down, total = small_call(far_kernel, (sent, sent, piece), "far_parts", below, above, gram, gram_other)
    far_up, far_down = bar((shift(to_up, distance=STRIDE), shift(to_down, distance=-STRIDE)))
    farthest = shift(far_up[half:], distance=STRIDE)
    pack = small_call(
        pack_kernel, half_rows(pack_rows + 2 * share), "pack", own, below, above, far_up, far_down, total, farthest
    )

    gathered = [pack]
    up, down = pack, pack
    for hop in range(HOPS + 1):
        last = hop == HOPS
        up = shift(up[pack_rows // 2 :] if last else up, distance=1)
        down = shift(down[pack_rows // 2 : pack_rows] if last else down, distance=-1)
        up, down = bar((up, down))
        gathered += [up, down]
    near = join(gathered, [pack_rows] * (2 * HOPS + 1) + [pack_rows // 2] * 2)
    other = core_swap(near, chips)

    spread = small_call(
        spread_kernel, jax.ShapeDtypeStruct((replicas, share, features), jnp.float32), "spread", *gathered[:-1]
    )
    gram = lax.all_to_all(spread.reshape(features, features), "rep", 0, 0, tiled=True)

    owned = owned_rows // UROWS
    places = pool_places(tile_users, chips, replicas, owned)
    weight = item_weights(tile_counts, item_factors.shape[0] // IBLK)
    rows, started = first_residue(places, [near, other], weight, item_factors)
    return solve_steps(rows, weight, item_factors, started, gram)


def solution(mesh):
    in_specs = (
        P(("grp", "rep"), None),
        P(("grp", "rep"), None),
        P(("grp", "rep")),
        P(("grp", "rep"), None, None),
    )
    out_specs = P(("grp", "rep"), None)
    return jax.shard_map(
        on_device, mesh=mesh, in_specs=in_specs, out_specs=out_specs, check_vma=False
    )
```

```python
import functools

import jax
import jax.numpy as jnp
import numpy as np
from jax import lax
from jax.experimental import pallas as pl
from jax.experimental.pallas import tpu as pltpu
from jax.sharding import PartitionSpec as P

UROWS = 64
IBLK = 128
ITERS = 3
CORES = 2
HOPS = 3
STRIDE = 2 * HOPS + 1
CHUNK = 256
MIB = 1024 * 1024

ALPHA = 8.0
LAMBDA = 1.0
EPSILON = 1e-06


def chip_shift(value, chips, distance):
    pairs = [
        (CORES * chip + core, CORES * ((chip + (1 - 2 * core) * distance) % chips) + core)
        for chip in range(chips)
        for core in range(CORES)
    ]
    return lax.ppermute(value, "grp", pairs)


def core_swap(value, chips):
    pairs = [(CORES * chip + core, CORES * chip + 1 - core) for chip in range(chips) for core in range(CORES)]
    return lax.ppermute(value, "grp", pairs)


def slot_table(chips):
    slots = [0, -STRIDE, STRIDE, -2 * STRIDE, 2 * STRIDE]
    order = [slot - hop for hop in range(HOPS + 1) for slot in slots]
    order += [slot + hop for hop in range(1, HOPS + 1) for slot in slots[:-1]]
    table = np.full((chips,), -1, np.int32)
    for place, distance in enumerate(order):
        table[distance % chips] = place
    assert len(order) == chips and (table >= 0).all()
    return table


def pool_places(tile_users, chips, replicas, owned):
    member = tile_users // (owned * replicas)
    core = member % CORES
    here = lax.axis_index("grp")
    ahead = ((1 - 2 * core) * (member // CORES - here // CORES) + chips) % chips
    distances = np.arange(chips, dtype=np.int32)
    slot = jnp.sum(jnp.where(ahead[:, None] == distances, slot_table(chips), 0), axis=1)
    other_core = (core != here % CORES).astype(jnp.int32)
    return ((other_core * chips + slot) * owned + tile_users % owned).astype(jnp.int32)


def merge(parts):
    half = parts.shape[0] // 2
    return parts[:half].astype(jnp.float32) + parts[half:].astype(jnp.float32)


def dot(left, right):
    return jnp.dot(left, right, preferred_element_type=jnp.float32)


def dot_turned(left, right):
    return lax.dot_general(left, right, (((1,), (1,)), ((), ())), preferred_element_type=jnp.float32)


def high_low(value):
    high = value.astype(jnp.bfloat16)
    return high, (value - high.astype(jnp.float32)).astype(jnp.bfloat16)


def item_rows(block):
    return slice(block * IBLK, (block + 1) * IBLK)


SCALAR = pl.BlockSpec(memory_space=pltpu.SMEM)
VECTOR = pl.BlockSpec(memory_space=pltpu.VMEM)


def small_call(kernel, outs, name, *args):
    return pl.pallas_call(
        kernel,
        out_shape=outs,
        in_specs=[VECTOR] * len(args),
        out_specs=jax.tree.map(lambda _: VECTOR, outs),
        compiler_params=pltpu.CompilerParams(vmem_limit_bytes=8 * MIB),
        name=name,
    )(*args)


def gram_kernel(users_ref, gram_ref, own_ref):
    high, low = high_low(users_ref[...])
    own_ref[...] = high
    dims = (((0,), (0,)), ((), ()))
    product = functools.partial(lax.dot_general, dimension_numbers=dims, preferred_element_type=jnp.float32)
    gram_ref[...] = product(high, high) + (product(high, low) + product(low, high))


def weight_kernel(counts_ref, weight_ref):
    blocks, _, depth = weight_ref.shape
    tiles = IBLK // UROWS
    for block in range(blocks):
        for start in range(0, depth, IBLK):
            first = (block * depth + start) // UROWS
            counts = counts_ref[first : first + tiles].reshape(IBLK, IBLK).astype(jnp.float32)
            weight_ref[block, :, start : start + IBLK] = (ALPHA * counts).T.astype(jnp.bfloat16)


def tile_part(total, high, block, rows_ref, weight_ref):
    depth = weight_ref.shape[2]
    for start in range(0, depth, CHUNK):
        rows = rows_ref[block * depth + start : block * depth + start + CHUNK, :]
        scores = dot_turned(high, rows)
        weight = weight_ref[block, :, start : start + CHUNK].astype(jnp.float32)
        total = total + dot((weight * scores).astype(jnp.bfloat16), rows)
    return total


def first_kernel(places_ref, *refs):
    gathered, (weight_ref, items_ref, rows_ref, residue_ref, pool_ref) = refs[:-5], refs[-5:]
    filled = 0
    for part in gathered:
        pool_ref[filled : filled + part.shape[0], :] = part[...]
        filled += part.shape[0]

    def fetch(tile, carry):
        to = pl.ds(pl.multiple_of(tile * UROWS, UROWS), UROWS)
        at = pl.ds(pl.multiple_of(places_ref[tile] * UROWS, UROWS), UROWS)
        rows_ref[to, :] = pool_ref[at, :]
        return carry

    lax.fori_loop(0, places_ref.shape[0], fetch, 0, unroll=4)
    blocks, _, depth = weight_ref.shape
    for block in range(blocks):
        guess = items_ref[item_rows(block), :]
        target = -LAMBDA * guess
        for start in range(0, depth, CHUNK):
            weight = weight_ref[block, :, start : start + CHUNK]
            confidence = weight + jnp.where(weight > 0, 1.0, 0.0).astype(jnp.bfloat16)
            target = target + dot(confidence, rows_ref[block * depth + start : block * depth + start + CHUNK, :])
        part = tile_part(jnp.zeros_like(guess), guess.astype(jnp.bfloat16), block, rows_ref, weight_ref)
        residue_ref[item_rows(block), :] = target - part


def first_residue(places, gathered, weight, items):
    blocks, _, depth = weight.shape
    features = items.shape[1]
    pool_rows = sum(part.shape[0] for part in gathered)
    return pl.pallas_call(
        first_kernel,
        out_shape=(
            jax.ShapeDtypeStruct((blocks * depth, features), jnp.bfloat16),
            jax.ShapeDtypeStruct(items.shape, jnp.float32),
        ),
        in_specs=[SCALAR] + [VECTOR] * (len(gathered) + 2),
        out_specs=(VECTOR, VECTOR),
        scratch_shapes=[pltpu.VMEM((pool_rows, features), jnp.bfloat16)],
        compiler_params=pltpu.CompilerParams(vmem_limit_bytes=20 * MIB),
        name="first_residue",
    )(places, *gathered, weight, items)


def steps_kernel(
    rows_ref, weight_ref, items_ref, started_ref, gram_ref, guess_ref, high_ref, low_ref, residue_ref, direction_ref,
    applied_ref,
):
    blocks = weight_ref.shape[0]
    high_ref[...], low_ref[...] = high_low(gram_ref[...])

    def gram_part(vector):
        high, low = high_low(vector)
        return dot(high, high_ref[...]) + (dot(high, low_ref[...]) + dot(low, high_ref[...]))

    guess = items_ref[...]
    guess_ref[...] = guess
    residue = started_ref[...] - gram_part(guess)
    residue_ref[...] = residue
    direction_ref[...] = residue

    def step(iteration, current):
        vector = direction_ref[...]
        applied_ref[...] = vector * LAMBDA + gram_part(vector)
        for block in range(blocks):
            span = item_rows(block)
            high = direction_ref[span, :].astype(jnp.bfloat16)
            applied_ref[span, :] = tile_part(applied_ref[span, :], high, block, rows_ref, weight_ref)
        direction = direction_ref[...]
        applied = applied_ref[...]
        size = current / (jnp.sum(direction * applied, axis=1, keepdims=True) + EPSILON)
        guess_ref[...] += size * direction
        residue = residue_ref[...] - size * applied
        residue_ref[...] = residue
        following = jnp.sum(residue * residue, axis=1, keepdims=True)
        direction_ref[...] = residue + (following / (current + EPSILON)) * direction
        return following

    lax.fori_loop(0, ITERS, step, jnp.sum(residue * residue, axis=1, keepdims=True))


def solve_steps(rows, weight, items, started, gram):
    features = items.shape[1]
    state = pltpu.VMEM(items.shape, jnp.float32)
    square = pltpu.VMEM((features, features), jnp.bfloat16)
    return pl.pallas_call(
        steps_kernel,
        out_shape=jax.ShapeDtypeStruct(items.shape, jnp.float32),
        in_specs=[VECTOR] * 5,
        out_specs=VECTOR,
        scratch_shapes=[square, square, state, state, state],
        compiler_params=pltpu.CompilerParams(vmem_limit_bytes=16 * MIB),
        name="solve_steps",
    )(rows, weight, items, started, gram)


def put_parts(ref, start, value):
    count = value.shape[0]
    ref[start : start + count, :], ref[start + count : start + 2 * count, :] = high_low(value)


def own_kernel(own_ref, mine_ref, other_ref, out_ref):
    rows = own_ref.shape[0]
    out_ref[:rows, :] = own_ref[...]
    put_parts(out_ref, rows, mine_ref[...] + other_ref[...])


def pack_kernel(rows, *refs):
    parts, (up_ref, down_ref) = refs[:-2], refs[-2:]
    total = None
    for place, part in enumerate(parts):
        up_ref[place * rows : (place + 1) * rows, :] = part[:rows, :]
        if place < len(parts) - 1:
            down_ref[place * rows : (place + 1) * rows, :] = part[:rows, :]
        else:
            put_parts(down_ref, place * rows, total)
        piece = merge(part[rows:, :])
        total = piece if total is None else total + piece
    put_parts(up_ref, len(parts) * rows, total)


def join_kernel(counts, *refs):
    filled = 0
    for count, part in zip(counts, refs[:-1]):
        refs[-1][filled : filled + count, :] = part[:count, :]
        filled += count


def join(parts, counts):
    out = jax.ShapeDtypeStruct((sum(counts), parts[0].shape[1]), parts[0].dtype)
    return small_call(functools.partial(join_kernel, counts), out, "join", *parts)


def spread_kernel(*refs):
    parts, out_ref = refs[:-1], refs[-1]
    copies, share, _ = out_ref.shape
    total = functools.reduce(jnp.add, [merge(part[-2 * share :, :]) for part in parts])
    for copy in range(copies):
        out_ref[copy] = total


def on_device(user_factors, item_factors, tile_users, tile_counts):
    chips = lax.axis_size("grp") // CORES
    replicas = lax.axis_size("rep")
    owned_rows, features = user_factors.shape
    blocks = item_factors.shape[0] // IBLK
    share = features // replicas
    parts = 2 * share
    shift = functools.partial(chip_shift, chips=chips)
    bar = lax.optimization_barrier

    def half_rows(count):
        return jax.ShapeDtypeStruct((count, features), jnp.bfloat16)

    square = jax.ShapeDtypeStruct((features, features), jnp.float32)
    gram, own = small_call(gram_kernel, (square, half_rows(owned_rows)), "local_gram", user_factors)
    pieces = lax.all_to_all(gram, "rep", 0, 0, tiled=True)
    gram = jnp.sum(pieces.reshape(replicas, share, features), axis=0)
    own = small_call(own_kernel, half_rows(owned_rows + parts), "own", own, gram, core_swap(gram, chips))

    below, above = bar((shift(own, distance=STRIDE), shift(own, distance=-STRIDE)))
    far_below, far_above = bar((shift(below, distance=STRIDE), shift(above, distance=-STRIDE)))
    up, down = small_call(
        functools.partial(pack_kernel, owned_rows),
        (half_rows(5 * owned_rows + parts), half_rows(4 * owned_rows + parts)),
        "pack",
        own,
        below,
        above,
        far_below,
        far_above,
    )
    ups, downs = [up], []
    weight = small_call(
        weight_kernel,
        jax.ShapeDtypeStruct((blocks, IBLK, tile_counts.shape[0] * UROWS // blocks), jnp.bfloat16),
        "item_weights",
        tile_counts,
    )
    places = pool_places(tile_users, chips, replicas, owned_rows // UROWS)
    for hop in range(HOPS):
        up, down = shift(up, distance=1), shift(down, distance=-1)
        if hop == 0:
            up, down, weight, places = bar((up, down, weight, places))
        else:
            up, down = bar((up, down))
        ups.append(up)
        downs.append(down)

    near = join(ups + downs, [5 * owned_rows] * (HOPS + 1) + [4 * owned_rows] * HOPS)
    other = core_swap(near, chips)
    spread = small_call(
        spread_kernel, jax.ShapeDtypeStruct((replicas, share, features), jnp.float32), "spread", *ups, *downs
    )
    gram = lax.all_to_all(spread.reshape(features, features), "rep", 0, 0, tiled=True)
    rows, started = first_residue(places, [near, other], weight, item_factors)
    return solve_steps(rows, weight, item_factors, started, gram)


def solution(mesh):
    in_specs = (
        P(("grp", "rep"), None),
        P(("grp", "rep"), None),
        P(("grp", "rep")),
        P(("grp", "rep"), None, None),
    )
    out_specs = P(("grp", "rep"), None)
    return jax.shard_map(
        on_device, mesh=mesh, in_specs=in_specs, out_specs=out_specs, check_vma=False
    )
```

```python
import functools

import jax
import jax.numpy as jnp
import numpy as np
from jax import lax
from jax.experimental import pallas as pl
from jax.experimental.pallas import tpu as pltpu
from jax.sharding import PartitionSpec as P

UROWS = 64
IBLK = 128
ITERS = 3
CORES = 2
HOPS = 3
STRIDE = 2 * HOPS + 1
CHUNK = 256
MIB = 1024 * 1024

ALPHA = 8.0
LAMBDA = 1.0
EPSILON = 1e-06


def chip_shift(value, chips, distance):
    pairs = [
        (CORES * chip + core, CORES * ((chip + (1 - 2 * core) * distance) % chips) + core)
        for chip in range(chips)
        for core in range(CORES)
    ]
    return lax.ppermute(value, "grp", pairs)


def core_swap(value, chips):
    pairs = [(CORES * chip + core, CORES * chip + 1 - core) for chip in range(chips) for core in range(CORES)]
    return lax.ppermute(value, "grp", pairs)


def slot_table(chips):
    slots = [0, -STRIDE, STRIDE, -2 * STRIDE, 2 * STRIDE]
    order = [slot - hop for hop in range(HOPS + 1) for slot in slots]
    order += [slot + hop for hop in range(1, HOPS + 1) for slot in slots[:-1]]
    table = np.full((chips,), -1, np.int32)
    for place, distance in enumerate(order):
        table[distance % chips] = place
    assert len(order) == chips and (table >= 0).all()
    return table


def pool_places(tile_users, chips, replicas, owned):
    member = tile_users // (owned * replicas)
    core = member % CORES
    here = lax.axis_index("grp")
    ahead = ((1 - 2 * core) * (member // CORES - here // CORES) + chips) % chips
    distances = np.arange(chips, dtype=np.int32)
    slot = jnp.sum(jnp.where(ahead[:, None] == distances, slot_table(chips), 0), axis=1)
    other_core = (core != here % CORES).astype(jnp.int32)
    return ((other_core * chips + slot) * owned + tile_users % owned).astype(jnp.int32)


def merge(parts):
    half = parts.shape[0] // 2
    return parts[:half].astype(jnp.float32) + parts[half:].astype(jnp.float32)


def dot(left, right):
    return jnp.dot(left, right, preferred_element_type=jnp.float32)


def dot_turned(left, right):
    return lax.dot_general(left, right, (((1,), (1,)), ((), ())), preferred_element_type=jnp.float32)


def high_low(value):
    high = value.astype(jnp.bfloat16)
    return high, (value - high.astype(jnp.float32)).astype(jnp.bfloat16)


def item_rows(block):
    return slice(block * IBLK, (block + 1) * IBLK)


SCALAR = pl.BlockSpec(memory_space=pltpu.SMEM)
VECTOR = pl.BlockSpec(memory_space=pltpu.VMEM)
OUTER = pl.BlockSpec(memory_space=pltpu.HBM)


def outer(value):
    return pltpu.with_memory_space_constraint(value, pltpu.HBM)


def small_call(kernel, outs, name, *args):
    return pl.pallas_call(
        kernel,
        out_shape=outs,
        in_specs=[VECTOR] * len(args),
        out_specs=jax.tree.map(lambda _: VECTOR, outs),
        compiler_params=pltpu.CompilerParams(vmem_limit_bytes=8 * MIB),
        name=name,
    )(*args)


def gram_kernel(users_ref, gram_ref, own_ref):
    high, low = high_low(users_ref[...])
    own_ref[...] = high
    dims = (((0,), (0,)), ((), ()))
    product = functools.partial(lax.dot_general, dimension_numbers=dims, preferred_element_type=jnp.float32)
    gram_ref[...] = product(high, high) + (product(high, low) + product(low, high))


def weight_kernel(counts_ref, weight_ref):
    blocks, _, depth = weight_ref.shape
    tiles = IBLK // UROWS
    for block in range(blocks):
        for start in range(0, depth, IBLK):
            first = (block * depth + start) // UROWS
            counts = counts_ref[first : first + tiles].reshape(IBLK, IBLK).astype(jnp.float32)
            weight_ref[block, :, start : start + IBLK] = (ALPHA * counts).T.astype(jnp.bfloat16)


def tile_part(total, high, block, rows_ref, weight_ref):
    depth = weight_ref.shape[2]
    for start in range(0, depth, CHUNK):
        rows = rows_ref[block * depth + start : block * depth + start + CHUNK, :]
        scores = dot_turned(high, rows)
        weight = weight_ref[block, :, start : start + CHUNK].astype(jnp.float32)
        total = total + dot((weight * scores).astype(jnp.bfloat16), rows)
    return total


def first_kernel(
    places_ref, near_ref, other_ref, weight_in_ref, items_in_ref, rows_out_ref, started_out_ref, rows_ref, weight_ref,
    items_ref, started_ref, sems,
):
    near_blocks = near_ref.shape[0] // UROWS
    bring_weight = pltpu.make_async_copy(weight_in_ref, weight_ref, sems.at[0])
    bring_items = pltpu.make_async_copy(items_in_ref, items_ref, sems.at[1])
    bring_weight.start()
    bring_items.start()

    def fetch(tile, carry):
        place = places_ref[tile]
        to = rows_ref.at[pl.ds(pl.multiple_of(tile * UROWS, UROWS), UROWS), :]

        @pl.when(place < near_blocks)
        def _():
            at = pl.ds(pl.multiple_of(place * UROWS, UROWS), UROWS)
            pltpu.make_async_copy(near_ref.at[at, :], to, sems.at[2]).start()

        @pl.when(place >= near_blocks)
        def _():
            at = pl.ds(pl.multiple_of((place - near_blocks) * UROWS, UROWS), UROWS)
            pltpu.make_async_copy(other_ref.at[at, :], to, sems.at[2]).start()

        return carry

    lax.fori_loop(0, places_ref.shape[0], fetch, 0)
    bring_weight.wait()
    bring_items.wait()
    pltpu.make_async_copy(rows_ref, rows_ref, sems.at[2]).wait()
    keep_rows = pltpu.make_async_copy(rows_ref, rows_out_ref, sems.at[3])
    keep_rows.start()
    blocks, _, depth = weight_ref.shape
    for block in range(blocks):
        guess = items_ref[item_rows(block), :]
        target = -LAMBDA * guess
        for start in range(0, depth, CHUNK):
            weight = weight_ref[block, :, start : start + CHUNK]
            confidence = weight + jnp.where(weight > 0, 1.0, 0.0).astype(jnp.bfloat16)
            target = target + dot(confidence, rows_ref[block * depth + start : block * depth + start + CHUNK, :])
        part = tile_part(jnp.zeros_like(guess), guess.astype(jnp.bfloat16), block, rows_ref, weight_ref)
        started_ref[item_rows(block), :] = target - part
    keep_started = pltpu.make_async_copy(started_ref, started_out_ref, sems.at[4])
    keep_started.start()
    keep_started.wait()
    keep_rows.wait()


def first_residue(places, near, other, weight, items):
    blocks, _, depth = weight.shape
    rows = (blocks * depth, items.shape[1])
    return pl.pallas_call(
        first_kernel,
        out_shape=(pltpu.HBM(rows, jnp.bfloat16), pltpu.HBM(items.shape, jnp.float32)),
        in_specs=[SCALAR, OUTER, pl.BlockSpec(memory_space=pl.ANY), OUTER, OUTER],
        out_specs=(OUTER, OUTER),
        scratch_shapes=[
            pltpu.VMEM(rows, jnp.bfloat16),
            pltpu.VMEM(weight.shape, jnp.bfloat16),
            pltpu.VMEM(items.shape, jnp.float32),
            pltpu.VMEM(items.shape, jnp.float32),
            pltpu.SemaphoreType.DMA((5,)),
        ],
        compiler_params=pltpu.CompilerParams(vmem_limit_bytes=12 * MIB),
        name="first_residue",
    )(places, outer(near), other, outer(weight), outer(items))


def steps_kernel(
    rows_in_ref, weight_in_ref, items_ref, started_ref, gram_ref, guess_ref, rows_ref, weight_ref, high_ref, low_ref,
    residue_ref, direction_ref, applied_ref, sems,
):
    sources = (items_ref, started_ref, weight_in_ref, rows_in_ref)
    places = (guess_ref, residue_ref, weight_ref, rows_ref)
    copies = [pltpu.make_async_copy(*pair, sems.at[at]) for at, pair in enumerate(zip(sources, places))]
    for copy in copies:
        copy.start()
    blocks = weight_ref.shape[0]
    high_ref[...], low_ref[...] = high_low(gram_ref[...])

    def gram_part(vector):
        high, low = high_low(vector)
        return dot(high, high_ref[...]) + (dot(high, low_ref[...]) + dot(low, high_ref[...]))

    copies[0].wait()
    copies[1].wait()
    residue = residue_ref[...] - gram_part(guess_ref[...])
    residue_ref[...] = residue
    direction_ref[...] = residue
    copies[2].wait()
    copies[3].wait()

    def step(iteration, current):
        vector = direction_ref[...]
        applied_ref[...] = vector * LAMBDA + gram_part(vector)
        for block in range(blocks):
            span = item_rows(block)
            high = direction_ref[span, :].astype(jnp.bfloat16)
            applied_ref[span, :] = tile_part(applied_ref[span, :], high, block, rows_ref, weight_ref)
        direction = direction_ref[...]
        applied = applied_ref[...]
        size = current / (jnp.sum(direction * applied, axis=1, keepdims=True) + EPSILON)
        guess_ref[...] += size * direction
        residue = residue_ref[...] - size * applied
        residue_ref[...] = residue
        following = jnp.sum(residue * residue, axis=1, keepdims=True)
        direction_ref[...] = residue + (following / (current + EPSILON)) * direction
        return following

    lax.fori_loop(0, ITERS, step, jnp.sum(residue * residue, axis=1, keepdims=True))


def solve_steps(rows, weight, items, started, gram):
    features = items.shape[1]
    state = pltpu.VMEM(items.shape, jnp.float32)
    square = pltpu.VMEM((features, features), jnp.bfloat16)
    return pl.pallas_call(
        steps_kernel,
        out_shape=jax.ShapeDtypeStruct(items.shape, jnp.float32),
        in_specs=[OUTER] * 4 + [VECTOR],
        out_specs=VECTOR,
        scratch_shapes=[
            pltpu.VMEM(rows.shape, jnp.bfloat16),
            pltpu.VMEM(weight.shape, jnp.bfloat16),
            square,
            square,
            state,
            state,
            state,
            pltpu.SemaphoreType.DMA((4,)),
        ],
        compiler_params=pltpu.CompilerParams(vmem_limit_bytes=14 * MIB),
        name="solve_steps",
    )(*map(outer, (rows, weight, items, started)), gram)


def put_parts(ref, start, value):
    count = value.shape[0]
    ref[start : start + count, :], ref[start + count : start + 2 * count, :] = high_low(value)


def own_kernel(own_ref, mine_ref, other_ref, out_ref):
    rows = own_ref.shape[0]
    out_ref[:rows, :] = own_ref[...]
    put_parts(out_ref, rows, mine_ref[...] + other_ref[...])


def pack_kernel(rows, *refs):
    parts, (up_ref, down_ref) = refs[:-2], refs[-2:]
    total = None
    for place, part in enumerate(parts):
        up_ref[place * rows : (place + 1) * rows, :] = part[:rows, :]
        if place < len(parts) - 1:
            down_ref[place * rows : (place + 1) * rows, :] = part[:rows, :]
        else:
            put_parts(down_ref, place * rows, total)
        piece = merge(part[rows:, :])
        total = piece if total is None else total + piece
    put_parts(up_ref, len(parts) * rows, total)


def collect_kernel(rows, places, share, *refs):
    parts, (near_ref, total_ref, sems) = refs[: len(rows)], refs[-3:]
    copies = []
    for at, part in enumerate(parts):
        to = near_ref.at[places[at] : places[at] + rows[at], :]
        copies.append(pltpu.make_async_copy(part.at[: rows[at], :], to, sems.at[at]))
        copies[-1].start()
    total = functools.reduce(jnp.add, [merge(part[-2 * share :, :]) for part in parts])
    total_ref[...] = total if len(refs) == len(rows) + 3 else refs[len(rows) + 1][...] + total
    for copy in copies:
        copy.wait()


def collect(name, parts, rows, places, near_shape, share, *earlier):
    count = len(parts)
    return pl.pallas_call(
        functools.partial(collect_kernel, rows, places, share),
        out_shape=(near_shape, jax.ShapeDtypeStruct((share, near_shape.shape[1]), jnp.float32)),
        in_specs=[VECTOR] * count + [OUTER, VECTOR][: len(earlier)],
        out_specs=(OUTER, VECTOR),
        scratch_shapes=[pltpu.SemaphoreType.DMA((count,))],
        input_output_aliases={count: 0} if earlier else {},
        compiler_params=pltpu.CompilerParams(vmem_limit_bytes=4 * MIB),
        name=name,
    )(*parts, *map(outer, earlier[:1]), *earlier[1:])


def spread_kernel(total_ref, out_ref, copies_ref, sem):
    total = total_ref[...]
    for copy in range(copies_ref.shape[0]):
        copies_ref[copy] = total
    write = pltpu.make_async_copy(copies_ref, out_ref, sem)
    write.start()
    write.wait()


def spread(total, replicas):
    shape = (replicas,) + total.shape
    return pl.pallas_call(
        spread_kernel,
        out_shape=pltpu.HBM(shape, jnp.float32),
        in_specs=[VECTOR],
        out_specs=OUTER,
        scratch_shapes=[pltpu.VMEM(shape, jnp.float32), pltpu.SemaphoreType.DMA],
        compiler_params=pltpu.CompilerParams(vmem_limit_bytes=4 * MIB),
        name="spread",
    )(total)


def on_device(user_factors, item_factors, tile_users, tile_counts):
    chips = lax.axis_size("grp") // CORES
    replicas = lax.axis_size("rep")
    owned_rows, features = user_factors.shape
    blocks = item_factors.shape[0] // IBLK
    share = features // replicas
    parts = 2 * share
    shift = functools.partial(chip_shift, chips=chips)
    bar = lax.optimization_barrier

    def half_rows(count):
        return jax.ShapeDtypeStruct((count, features), jnp.bfloat16)

    square = jax.ShapeDtypeStruct((features, features), jnp.float32)
    gram, own = small_call(gram_kernel, (square, half_rows(owned_rows)), "local_gram", user_factors)
    pieces = lax.all_to_all(gram, "rep", 0, 0, tiled=True)
    gram = jnp.sum(pieces.reshape(replicas, share, features), axis=0)
    own = small_call(own_kernel, half_rows(owned_rows + parts), "own", own, gram, core_swap(gram, chips))

    below, above = bar((shift(own, distance=STRIDE), shift(own, distance=-STRIDE)))
    far_below, far_above = bar((shift(below, distance=STRIDE), shift(above, distance=-STRIDE)))
    up, down = small_call(
        functools.partial(pack_kernel, owned_rows),
        (half_rows(5 * owned_rows + parts), half_rows(4 * owned_rows + parts)),
        "pack",
        own,
        below,
        above,
        far_below,
        far_above,
    )
    weight = small_call(
        weight_kernel,
        jax.ShapeDtypeStruct((blocks, IBLK, tile_counts.shape[0] * UROWS // blocks), jnp.bfloat16),
        "item_weights",
        tile_counts,
    )
    places = pool_places(tile_users, chips, replicas, owned_rows // UROWS)
    up_rows, down_rows = 5 * owned_rows, 4 * owned_rows
    near_shape = pltpu.HBM((chips * owned_rows, features), jnp.bfloat16)
    near, total = collect("collect_0", [up], [up_rows], [0], near_shape, share)
    for hop in range(1, HOPS + 1):
        up, down = shift(up, distance=1), shift(down, distance=-1)
        if hop == 1:
            up, down, near, total, weight, places = bar((up, down, near, total, weight, places))
        else:
            up, down, near, total = bar((up, down, near, total))
        at = [hop * up_rows, (HOPS + 1) * up_rows + (hop - 1) * down_rows]
        near, total = collect("collect_" + str(hop), [up, down], [up_rows, down_rows], at, near_shape, share, near, total)

    other = core_swap(near, chips)
    gram = lax.all_to_all(spread(total, replicas).reshape(features, features), "rep", 0, 0, tiled=True)
    rows, started = first_residue(places, near, other, weight, item_factors)
    return solve_steps(rows, weight, item_factors, started, gram)


def solution(mesh):
    in_specs = (
        P(("grp", "rep"), None),
        P(("grp", "rep"), None),
        P(("grp", "rep")),
        P(("grp", "rep"), None, None),
    )
    out_specs = P(("grp", "rep"), None)
    return jax.shard_map(
        on_device, mesh=mesh, in_specs=in_specs, out_specs=out_specs, check_vma=False
    )
```

```python
import functools

import jax
import jax.numpy as jnp
import numpy as np
from jax import lax
from jax.experimental import pallas as pl
from jax.experimental.pallas import tpu as pltpu
from jax.sharding import PartitionSpec as P

UROWS = 64
IBLK = 128
ITERS = 3
CORES = 2
HOPS = 3
STRIDE = 2 * HOPS + 1
CHUNK = 256
MIB = 1024 * 1024

ALPHA = 8.0
LAMBDA = 1.0
EPSILON = 1e-06


def chip_shift(value, chips, distance):
    pairs = [
        (CORES * chip + core, CORES * ((chip + (1 - 2 * core) * distance) % chips) + core)
        for chip in range(chips)
        for core in range(CORES)
    ]
    return lax.ppermute(value, "grp", pairs)


def core_swap(value, chips):
    pairs = [(CORES * chip + core, CORES * chip + 1 - core) for chip in range(chips) for core in range(CORES)]
    return lax.ppermute(value, "grp", pairs)


def slot_table(chips):
    slots = [0, -STRIDE, STRIDE, -2 * STRIDE, 2 * STRIDE]
    order = [slot - hop for hop in range(HOPS + 1) for slot in slots]
    order += [slot + hop for hop in range(1, HOPS + 1) for slot in slots[:-1]]
    table = np.full((chips,), -1, np.int32)
    for place, distance in enumerate(order):
        table[distance % chips] = place
    assert len(order) == chips and (table >= 0).all()
    return table


def pool_places(tile_users, chips, replicas, owned):
    member = tile_users // (owned * replicas)
    core = member % CORES
    here = lax.axis_index("grp")
    ahead = ((1 - 2 * core) * (member // CORES - here // CORES) + chips) % chips
    distances = np.arange(chips, dtype=np.int32)
    slot = jnp.sum(jnp.where(ahead[:, None] == distances, slot_table(chips), 0), axis=1)
    other_core = (core != here % CORES).astype(jnp.int32)
    return ((other_core * chips + slot) * owned + tile_users % owned).astype(jnp.int32)


def merge(parts):
    half = parts.shape[0] // 2
    return parts[:half].astype(jnp.float32) + parts[half:].astype(jnp.float32)


def dot(left, right):
    return jnp.dot(left, right, preferred_element_type=jnp.float32)


def dot_turned(left, right):
    return lax.dot_general(left, right, (((1,), (1,)), ((), ())), preferred_element_type=jnp.float32)


def high_low(value):
    high = value.astype(jnp.bfloat16)
    return high, (value - high.astype(jnp.float32)).astype(jnp.bfloat16)


def item_rows(block):
    return slice(block * IBLK, (block + 1) * IBLK)


SCALAR = pl.BlockSpec(memory_space=pltpu.SMEM)
VECTOR = pl.BlockSpec(memory_space=pltpu.VMEM)
OUTER = pl.BlockSpec(memory_space=pltpu.HBM)


def outer(value):
    return pltpu.with_memory_space_constraint(value, pltpu.HBM)


def inner(value):
    return pltpu.with_memory_space_constraint(value, pltpu.VMEM)


def small_call(kernel, outs, name, *args):
    return pl.pallas_call(
        kernel,
        out_shape=outs,
        in_specs=[VECTOR] * len(args),
        out_specs=jax.tree.map(lambda _: VECTOR, outs),
        compiler_params=pltpu.CompilerParams(vmem_limit_bytes=8 * MIB),
        name=name,
    )(*args)


def gram_kernel(users_ref, gram_ref, own_ref):
    high, low = high_low(users_ref[...])
    own_ref[...] = high
    dims = (((0,), (0,)), ((), ()))
    product = functools.partial(lax.dot_general, dimension_numbers=dims, preferred_element_type=jnp.float32)
    gram_ref[...] = product(high, high) + (product(high, low) + product(low, high))


def weight_kernel(counts_ref, weight_ref):
    blocks, _, depth = weight_ref.shape
    tiles = IBLK // UROWS
    for block in range(blocks):
        for start in range(0, depth, IBLK):
            first = (block * depth + start) // UROWS
            counts = counts_ref[first : first + tiles].reshape(IBLK, IBLK).astype(jnp.float32)
            weight_ref[block, :, start : start + IBLK] = (ALPHA * counts).T.astype(jnp.bfloat16)


def tile_part(total, high, block, rows_ref, weight_ref):
    depth = weight_ref.shape[2]
    for start in range(0, depth, CHUNK):
        rows = rows_ref[block * depth + start : block * depth + start + CHUNK, :]
        scores = dot_turned(high, rows)
        weight = weight_ref[block, :, start : start + CHUNK].astype(jnp.float32)
        total = total + dot((weight * scores).astype(jnp.bfloat16), rows)
    return total


def first_kernel(
    places_ref, near_ref, other_ref, weight_ref, items_in_ref, open_rows_ref, rows_ref, started_out_ref, items_ref,
    started_ref, items_sem, sems, started_sems,
):
    del open_rows_ref
    near_blocks = near_ref.shape[0] // UROWS
    blocks, _, depth = weight_ref.shape
    per_block = depth // UROWS
    bring_items = pltpu.make_async_copy(items_in_ref, items_ref, items_sem)
    bring_items.start()

    def fetch(tile, block):
        place = places_ref[tile]
        to = rows_ref.at[pl.ds(pl.multiple_of(tile * UROWS, UROWS), UROWS), :]

        @pl.when(place < near_blocks)
        def _():
            at = pl.ds(pl.multiple_of(place * UROWS, UROWS), UROWS)
            pltpu.make_async_copy(near_ref.at[at, :], to, sems.at[block]).start()

        @pl.when(place >= near_blocks)
        def _():
            at = pl.ds(pl.multiple_of((place - near_blocks) * UROWS, UROWS), UROWS)
            pltpu.make_async_copy(other_ref.at[at, :], to, sems.at[block]).start()

        return block

    for block in range(blocks):
        lax.fori_loop(block * per_block, (block + 1) * per_block, fetch, block)
    bring_items.wait()
    kept = []
    for block in range(blocks):
        mine = rows_ref.at[block * depth : (block + 1) * depth, :]
        pltpu.make_async_copy(mine, mine, sems.at[block]).wait()
        guess = items_ref[item_rows(block), :]
        target = -LAMBDA * guess
        for start in range(0, depth, CHUNK):
            weight = weight_ref[block, :, start : start + CHUNK]
            confidence = weight + jnp.where(weight > 0, 1.0, 0.0).astype(jnp.bfloat16)
            target = target + dot(confidence, rows_ref[block * depth + start : block * depth + start + CHUNK, :])
        part = tile_part(jnp.zeros_like(guess), guess.astype(jnp.bfloat16), block, rows_ref, weight_ref)
        started_ref[item_rows(block), :] = target - part
        span = item_rows(block)
        kept.append(
            pltpu.make_async_copy(started_ref.at[span, :], started_out_ref.at[span, :], started_sems.at[block])
        )
        kept[-1].start()
    for copy in kept:
        copy.wait()


def first_residue(places, near, other, weight, items, rows):
    blocks = weight.shape[0]
    return pl.pallas_call(
        first_kernel,
        out_shape=(pltpu.VMEM(rows.shape, rows.dtype), pltpu.HBM(items.shape, jnp.float32)),
        in_specs=[SCALAR, OUTER, pl.BlockSpec(memory_space=pl.ANY), VECTOR, OUTER, VECTOR],
        out_specs=(VECTOR, OUTER),
        scratch_shapes=[
            pltpu.VMEM(items.shape, jnp.float32),
            pltpu.VMEM(items.shape, jnp.float32),
            pltpu.SemaphoreType.DMA,
            pltpu.SemaphoreType.DMA((blocks,)),
            pltpu.SemaphoreType.DMA((blocks,)),
        ],
        compiler_params=pltpu.CompilerParams(vmem_limit_bytes=8 * MIB),
        input_output_aliases={5: 0},
        name="first_residue",
    )(places, outer(near), other, inner(weight), outer(items), inner(rows))


def steps_kernel(
    rows_ref, weight_ref, items_ref, started_ref, gram_ref, guess_ref, high_ref, low_ref, residue_ref, direction_ref,
    applied_ref, sems,
):
    bring_items = pltpu.make_async_copy(items_ref, guess_ref, sems.at[0])
    bring_items.start()
    bring_started = pltpu.make_async_copy(started_ref, residue_ref, sems.at[1])
    bring_started.start()
    blocks = weight_ref.shape[0]
    high_ref[...], low_ref[...] = high_low(gram_ref[...])

    def gram_part(vector):
        high, low = high_low(vector)
        return dot(high, high_ref[...]) + (dot(high, low_ref[...]) + dot(low, high_ref[...]))

    bring_items.wait()
    first = gram_part(guess_ref[...])
    bring_started.wait()
    residue = residue_ref[...] - first
    residue_ref[...] = residue
    direction_ref[...] = residue

    def step(iteration, current):
        vector = direction_ref[...]
        applied_ref[...] = vector * LAMBDA + gram_part(vector)
        for block in range(blocks):
            span = item_rows(block)
            high = direction_ref[span, :].astype(jnp.bfloat16)
            applied_ref[span, :] = tile_part(applied_ref[span, :], high, block, rows_ref, weight_ref)
        direction = direction_ref[...]
        applied = applied_ref[...]
        size = current / (jnp.sum(direction * applied, axis=1, keepdims=True) + EPSILON)
        guess_ref[...] += size * direction
        residue = residue_ref[...] - size * applied
        residue_ref[...] = residue
        following = jnp.sum(residue * residue, axis=1, keepdims=True)
        direction_ref[...] = residue + (following / (current + EPSILON)) * direction
        return following

    lax.fori_loop(0, ITERS, step, jnp.sum(residue * residue, axis=1, keepdims=True))


def solve_steps(rows, weight, items, started, gram):
    features = items.shape[1]
    state = pltpu.VMEM(items.shape, jnp.float32)
    square = pltpu.VMEM((features, features), jnp.bfloat16)
    return pl.pallas_call(
        steps_kernel,
        out_shape=jax.ShapeDtypeStruct(items.shape, jnp.float32),
        in_specs=[VECTOR, VECTOR, OUTER, OUTER, VECTOR],
        out_specs=VECTOR,
        scratch_shapes=[square, square, state, state, state, pltpu.SemaphoreType.DMA((2,))],
        compiler_params=pltpu.CompilerParams(vmem_limit_bytes=10 * MIB),
        name="solve_steps",
    )(inner(rows), inner(weight), outer(items), outer(started), gram)


def put_parts(ref, start, value):
    count = value.shape[0]
    ref[start : start + count, :], ref[start + count : start + 2 * count, :] = high_low(value)


def own_kernel(own_ref, mine_ref, other_ref, out_ref):
    rows = own_ref.shape[0]
    out_ref[:rows, :] = own_ref[...]
    put_parts(out_ref, rows, mine_ref[...] + other_ref[...])


def pack_kernel(rows, *refs):
    parts, (up_ref, down_ref) = refs[:-2], refs[-2:]
    total = None
    for place, part in enumerate(parts):
        up_ref[place * rows : (place + 1) * rows, :] = part[:rows, :]
        if place < len(parts) - 1:
            down_ref[place * rows : (place + 1) * rows, :] = part[:rows, :]
        else:
            put_parts(down_ref, place * rows, total)
        piece = merge(part[rows:, :])
        total = piece if total is None else total + piece
    put_parts(up_ref, len(parts) * rows, total)


def collect_kernel(rows, places, share, *refs):
    parts, (near_ref, total_ref, sems) = refs[: len(rows)], refs[-3:]
    copies = []
    for at, part in enumerate(parts):
        to = near_ref.at[places[at] : places[at] + rows[at], :]
        copies.append(pltpu.make_async_copy(part.at[: rows[at], :], to, sems.at[at]))
        copies[-1].start()
    total = functools.reduce(jnp.add, [merge(part[-2 * share :, :]) for part in parts])
    total_ref[...] = total if len(refs) == len(rows) + 3 else refs[len(rows) + 1][...] + total
    for copy in copies:
        copy.wait()


def collect(name, parts, rows, places, near_shape, share, *earlier):
    count = len(parts)
    return pl.pallas_call(
        functools.partial(collect_kernel, rows, places, share),
        out_shape=(near_shape, jax.ShapeDtypeStruct((share, near_shape.shape[1]), jnp.float32)),
        in_specs=[VECTOR] * count + [OUTER, VECTOR][: len(earlier)],
        out_specs=(OUTER, VECTOR),
        scratch_shapes=[pltpu.SemaphoreType.DMA((count,))],
        input_output_aliases={count: 0} if earlier else {},
        compiler_params=pltpu.CompilerParams(vmem_limit_bytes=4 * MIB),
        name=name,
    )(*parts, *map(outer, earlier[:1]), *earlier[1:])


def spread_kernel(total_ref, out_ref, rows_ref, copies_ref, sem):
    del rows_ref
    total = total_ref[...]
    for copy in range(copies_ref.shape[0]):
        copies_ref[copy] = total
    write = pltpu.make_async_copy(copies_ref, out_ref, sem)
    write.start()
    write.wait()


def spread(total, replicas, rows_shape):
    shape = (replicas,) + total.shape
    return pl.pallas_call(
        spread_kernel,
        out_shape=(pltpu.HBM(shape, jnp.float32), pltpu.VMEM(rows_shape, jnp.bfloat16)),
        in_specs=[VECTOR],
        out_specs=(OUTER, VECTOR),
        scratch_shapes=[pltpu.VMEM(shape, jnp.float32), pltpu.SemaphoreType.DMA],
        compiler_params=pltpu.CompilerParams(vmem_limit_bytes=4 * MIB),
        name="spread",
    )(total)


def on_device(user_factors, item_factors, tile_users, tile_counts):
    chips = lax.axis_size("grp") // CORES
    replicas = lax.axis_size("rep")
    owned_rows, features = user_factors.shape
    blocks = item_factors.shape[0] // IBLK
    share = features // replicas
    parts = 2 * share
    shift = functools.partial(chip_shift, chips=chips)
    bar = lax.optimization_barrier

    def half_rows(count):
        return jax.ShapeDtypeStruct((count, features), jnp.bfloat16)

    square = jax.ShapeDtypeStruct((features, features), jnp.float32)
    gram, own = small_call(gram_kernel, (square, half_rows(owned_rows)), "local_gram", user_factors)
    pieces = lax.all_to_all(gram, "rep", 0, 0, tiled=True)
    gram = jnp.sum(pieces.reshape(replicas, share, features), axis=0)
    own = small_call(own_kernel, half_rows(owned_rows + parts), "own", own, gram, core_swap(gram, chips))

    below, above = shift(own, distance=STRIDE), shift(own, distance=-STRIDE)
    far_below, far_above = shift(below, distance=STRIDE), shift(above, distance=-STRIDE)
    up, down = small_call(
        functools.partial(pack_kernel, owned_rows),
        (half_rows(5 * owned_rows + parts), half_rows(4 * owned_rows + parts)),
        "pack",
        own,
        below,
        above,
        far_below,
        far_above,
    )
    weight = small_call(
        weight_kernel,
        pltpu.VMEM((blocks, IBLK, tile_counts.shape[0] * UROWS // blocks), jnp.bfloat16),
        "item_weights",
        tile_counts,
    )
    places = pool_places(tile_users, chips, replicas, owned_rows // UROWS)
    up_rows, down_rows = 5 * owned_rows, 4 * owned_rows
    near_shape = pltpu.HBM((chips * owned_rows, features), jnp.bfloat16)
    near, total = collect("collect_0", [up], [up_rows], [0], near_shape, share)
    for hop in range(1, HOPS + 1):
        up, down = shift(up, distance=1), shift(down, distance=-1)
        if hop == 1:
            up, near, total, weight, places = bar((up, near, total, weight, places))
        else:
            up, near, total = bar((up, near, total))
        at = [hop * up_rows, (HOPS + 1) * up_rows + (hop - 1) * down_rows]
        near, total = collect("collect_" + str(hop), [up, down], [up_rows, down_rows], at, near_shape, share, near, total)

    other = core_swap(near, chips)
    rows_shape = (tile_counts.shape[0] * UROWS, features)
    copies, rows = spread(total, replicas, rows_shape)
    gram = lax.all_to_all(copies.reshape(features, features), "rep", 0, 0, tiled=True)
    rows, started = first_residue(places, near, other, weight, item_factors, rows)
    return solve_steps(rows, weight, item_factors, started, gram)


def solution(mesh):
    in_specs = (
        P(("grp", "rep"), None),
        P(("grp", "rep"), None),
        P(("grp", "rep")),
        P(("grp", "rep"), None, None),
    )
    out_specs = P(("grp", "rep"), None)
    return jax.shard_map(
        on_device, mesh=mesh, in_specs=in_specs, out_specs=out_specs, check_vma=False
    )
```

```python
import functools

import jax
import jax.numpy as jnp
import numpy as np
from jax import lax
from jax.experimental import pallas as pl
from jax.experimental.pallas import tpu as pltpu
from jax.sharding import PartitionSpec as P

UROWS = 64
IBLK = 128
ITERS = 3
CORES = 2
HOPS = 3
STRIDE = 2 * HOPS + 1
CHUNK = 256
MIB = 1024 * 1024

ALPHA = 8.0
LAMBDA = 1.0
EPSILON = 1e-06


def chip_shift(value, chips, distance):
    pairs = [
        (CORES * chip + core, CORES * ((chip + (1 - 2 * core) * distance) % chips) + core)
        for chip in range(chips)
        for core in range(CORES)
    ]
    return lax.ppermute(value, "grp", pairs)


def core_swap(value, chips):
    pairs = [(CORES * chip + core, CORES * chip + 1 - core) for chip in range(chips) for core in range(CORES)]
    return lax.ppermute(value, "grp", pairs)


def slot_table(chips):
    slots = [0, -STRIDE, STRIDE, -2 * STRIDE, 2 * STRIDE]
    order = [slot - hop for hop in range(HOPS + 1) for slot in slots]
    order += [slot + hop for hop in range(1, HOPS + 1) for slot in slots[:-1]]
    table = np.full((chips,), -1, np.int32)
    for place, distance in enumerate(order):
        table[distance % chips] = place
    assert len(order) == chips and (table >= 0).all()
    return table


def pool_places(tile_users, chips, replicas, owned):
    member = tile_users // (owned * replicas)
    core = member % CORES
    here = lax.axis_index("grp")
    ahead = ((1 - 2 * core) * (member // CORES - here // CORES) + chips) % chips
    distances = np.arange(chips, dtype=np.int32)
    slot = jnp.sum(jnp.where(ahead[:, None] == distances, slot_table(chips), 0), axis=1)
    other_core = (core != here % CORES).astype(jnp.int32)
    return ((other_core * chips + slot) * owned + tile_users % owned).astype(jnp.int32)


def merge(parts):
    half = parts.shape[0] // 2
    return parts[:half].astype(jnp.float32) + parts[half:].astype(jnp.float32)


def dot(left, right):
    return jnp.dot(left, right, preferred_element_type=jnp.float32)


def dot_turned(left, right):
    return lax.dot_general(left, right, (((1,), (1,)), ((), ())), preferred_element_type=jnp.float32)


def high_low(value):
    high = value.astype(jnp.bfloat16)
    return high, (value - high.astype(jnp.float32)).astype(jnp.bfloat16)


def item_rows(block):
    return slice(block * IBLK, (block + 1) * IBLK)


SCALAR = pl.BlockSpec(memory_space=pltpu.SMEM)
VECTOR = pl.BlockSpec(memory_space=pltpu.VMEM)
OUTER = pl.BlockSpec(memory_space=pltpu.HBM)


def outer(value):
    return pltpu.with_memory_space_constraint(value, pltpu.HBM)


def inner(value):
    return pltpu.with_memory_space_constraint(value, pltpu.VMEM)


def small_call(kernel, outs, name, *args):
    return pl.pallas_call(
        kernel,
        out_shape=outs,
        in_specs=[VECTOR] * len(args),
        out_specs=jax.tree.map(lambda _: VECTOR, outs),
        compiler_params=pltpu.CompilerParams(vmem_limit_bytes=8 * MIB),
        name=name,
    )(*args)


def gram_kernel(users_ref, gram_ref, own_ref):
    high, low = high_low(users_ref[...])
    own_ref[...] = high
    dims = (((0,), (0,)), ((), ()))
    product = functools.partial(lax.dot_general, dimension_numbers=dims, preferred_element_type=jnp.float32)
    gram_ref[...] = product(high, high) + (product(high, low) + product(low, high))


def weight_kernel(counts_ref, weight_ref):
    blocks, _, depth = weight_ref.shape
    tiles = IBLK // UROWS
    for block in range(blocks):
        for start in range(0, depth, IBLK):
            first = (block * depth + start) // UROWS
            counts = counts_ref[first : first + tiles].reshape(IBLK, IBLK).astype(jnp.float32)
            weight_ref[block, :, start : start + IBLK] = (ALPHA * counts).T.astype(jnp.bfloat16)


def tile_part(total, high, block, rows_ref, weight_ref):
    depth = weight_ref.shape[2]
    for start in range(0, depth, CHUNK):
        rows = rows_ref[block * depth + start : block * depth + start + CHUNK, :]
        scores = dot_turned(high, rows)
        weight = weight_ref[block, :, start : start + CHUNK].astype(jnp.float32)
        total = total + dot((weight * scores).astype(jnp.bfloat16), rows)
    return total


def first_kernel(
    places_ref, near_ref, other_ref, weight_ref, items_in_ref, open_rows_ref, rows_ref, started_out_ref, items_ref,
    started_ref, items_sem, sems, started_sems,
):
    del open_rows_ref
    near_blocks = near_ref.shape[0] // UROWS
    blocks, _, depth = weight_ref.shape
    per_block = depth // UROWS
    bring_items = pltpu.make_async_copy(items_in_ref, items_ref, items_sem)
    bring_items.start()

    def fetch(tile, block):
        place = places_ref[tile]
        to = rows_ref.at[pl.ds(pl.multiple_of(tile * UROWS, UROWS), UROWS), :]

        @pl.when(place < near_blocks)
        def _():
            at = pl.ds(pl.multiple_of(place * UROWS, UROWS), UROWS)
            pltpu.make_async_copy(near_ref.at[at, :], to, sems.at[block]).start()

        @pl.when(place >= near_blocks)
        def _():
            at = pl.ds(pl.multiple_of((place - near_blocks) * UROWS, UROWS), UROWS)
            pltpu.make_async_copy(other_ref.at[at, :], to, sems.at[block]).start()

        return block

    for block in range(blocks):
        lax.fori_loop(block * per_block, (block + 1) * per_block, fetch, block)
    bring_items.wait()
    kept = []
    for block in range(blocks):
        mine = rows_ref.at[block * depth : (block + 1) * depth, :]
        pltpu.make_async_copy(mine, mine, sems.at[block]).wait()
        guess = items_ref[item_rows(block), :]
        target = -LAMBDA * guess
        for start in range(0, depth, CHUNK):
            weight = weight_ref[block, :, start : start + CHUNK]
            confidence = weight + jnp.where(weight > 0, 1.0, 0.0).astype(jnp.bfloat16)
            target = target + dot(confidence, rows_ref[block * depth + start : block * depth + start + CHUNK, :])
        part = tile_part(jnp.zeros_like(guess), guess.astype(jnp.bfloat16), block, rows_ref, weight_ref)
        started_ref[item_rows(block), :] = target - part
        span = item_rows(block)
        kept.append(
            pltpu.make_async_copy(started_ref.at[span, :], started_out_ref.at[span, :], started_sems.at[block])
        )
        kept[-1].start()
    for copy in kept:
        copy.wait()


def first_residue(places, near, other, weight, items, rows):
    blocks = weight.shape[0]
    return pl.pallas_call(
        first_kernel,
        out_shape=(pltpu.VMEM(rows.shape, rows.dtype), pltpu.HBM(items.shape, jnp.float32)),
        in_specs=[SCALAR, OUTER, pl.BlockSpec(memory_space=pl.ANY), VECTOR, OUTER, VECTOR],
        out_specs=(VECTOR, OUTER),
        scratch_shapes=[
            pltpu.VMEM(items.shape, jnp.float32),
            pltpu.VMEM(items.shape, jnp.float32),
            pltpu.SemaphoreType.DMA,
            pltpu.SemaphoreType.DMA((blocks,)),
            pltpu.SemaphoreType.DMA((blocks,)),
        ],
        compiler_params=pltpu.CompilerParams(vmem_limit_bytes=8 * MIB),
        input_output_aliases={5: 0},
        name="first_residue",
    )(places, outer(near), other, inner(weight), outer(items), inner(rows))


def steps_kernel(
    rows_ref, weight_ref, items_ref, started_ref, gram_ref, guess_ref, high_ref, low_ref, residue_ref, direction_ref,
    applied_ref, sems,
):
    bring_items = pltpu.make_async_copy(items_ref, guess_ref, sems.at[0])
    bring_items.start()
    bring_started = pltpu.make_async_copy(started_ref, residue_ref, sems.at[1])
    bring_started.start()
    blocks = weight_ref.shape[0]
    high_ref[...], low_ref[...] = high_low(gram_ref[...])

    def gram_part(vector):
        high, low = high_low(vector)
        return dot(high, high_ref[...]) + (dot(high, low_ref[...]) + dot(low, high_ref[...]))

    bring_items.wait()
    first = gram_part(guess_ref[...])
    bring_started.wait()
    residue = residue_ref[...] - first
    residue_ref[...] = residue
    direction_ref[...] = residue

    def step(iteration, current):
        vector = direction_ref[...]
        applied_ref[...] = vector * LAMBDA + gram_part(vector)
        for block in range(blocks):
            span = item_rows(block)
            high = direction_ref[span, :].astype(jnp.bfloat16)
            applied_ref[span, :] = tile_part(applied_ref[span, :], high, block, rows_ref, weight_ref)
        direction = direction_ref[...]
        applied = applied_ref[...]
        size = current / (jnp.sum(direction * applied, axis=1, keepdims=True) + EPSILON)
        guess_ref[...] += size * direction
        residue = residue_ref[...] - size * applied
        residue_ref[...] = residue
        following = jnp.sum(residue * residue, axis=1, keepdims=True)
        direction_ref[...] = residue + (following / (current + EPSILON)) * direction
        return following

    lax.fori_loop(0, ITERS, step, jnp.sum(residue * residue, axis=1, keepdims=True))


def solve_steps(rows, weight, items, started, gram):
    features = items.shape[1]
    state = pltpu.VMEM(items.shape, jnp.float32)
    square = pltpu.VMEM((features, features), jnp.bfloat16)
    return pl.pallas_call(
        steps_kernel,
        out_shape=jax.ShapeDtypeStruct(items.shape, jnp.float32),
        in_specs=[VECTOR, VECTOR, OUTER, OUTER, VECTOR],
        out_specs=VECTOR,
        scratch_shapes=[square, square, state, state, state, pltpu.SemaphoreType.DMA((2,))],
        compiler_params=pltpu.CompilerParams(vmem_limit_bytes=10 * MIB),
        name="solve_steps",
    )(inner(rows), inner(weight), outer(items), outer(started), gram)


def put_parts(ref, start, value):
    count = value.shape[0]
    ref[start : start + count, :], ref[start + count : start + 2 * count, :] = high_low(value)


def own_kernel(own_ref, mine_ref, other_ref, out_ref):
    rows = own_ref.shape[0]
    out_ref[:rows, :] = own_ref[...]
    put_parts(out_ref, rows, mine_ref[...] + other_ref[...])


def pack_kernel(rows, *refs):
    parts, (up_ref, down_ref) = refs[:-2], refs[-2:]
    total = None
    for place, part in enumerate(parts):
        up_ref[place * rows : (place + 1) * rows, :] = part[:rows, :]
        if place < len(parts) - 1:
            down_ref[place * rows : (place + 1) * rows, :] = part[:rows, :]
        else:
            put_parts(down_ref, place * rows, total)
        piece = merge(part[rows:, :])
        total = piece if total is None else total + piece
    put_parts(up_ref, len(parts) * rows, total)


def collect_kernel(rows, places, share, *refs):
    parts, (near_ref, total_ref, sems) = refs[: len(rows)], refs[-3:]
    copies = []
    for at, part in enumerate(parts):
        to = near_ref.at[places[at] : places[at] + rows[at], :]
        copies.append(pltpu.make_async_copy(part.at[: rows[at], :], to, sems.at[at]))
        copies[-1].start()
    total = functools.reduce(jnp.add, [merge(part[-2 * share :, :]) for part in parts])
    total_ref[...] = total if len(refs) == len(rows) + 3 else refs[len(rows) + 1][...] + total
    for copy in copies:
        copy.wait()


def collect(name, parts, rows, places, near_shape, share, *earlier):
    count = len(parts)
    return pl.pallas_call(
        functools.partial(collect_kernel, rows, places, share),
        out_shape=(near_shape, jax.ShapeDtypeStruct((share, near_shape.shape[1]), jnp.float32)),
        in_specs=[VECTOR] * count + [OUTER, VECTOR][: len(earlier)],
        out_specs=(OUTER, VECTOR),
        scratch_shapes=[pltpu.SemaphoreType.DMA((count,))],
        input_output_aliases={count: 0} if earlier else {},
        compiler_params=pltpu.CompilerParams(vmem_limit_bytes=4 * MIB),
        name=name,
    )(*parts, *map(outer, earlier[:1]), *earlier[1:])


def finish_kernel(rows, places, share, up_ref, down_ref, near_in_ref, total_ref, near_ref, out_ref, rows_ref, copies_ref, sems):
    del near_in_ref, rows_ref
    copies = []
    for at, part in enumerate((up_ref, down_ref)):
        to = near_ref.at[places[at] : places[at] + rows[at], :]
        copies.append(pltpu.make_async_copy(part.at[: rows[at], :], to, sems.at[at]))
        copies[-1].start()
    total = total_ref[...] + (merge(up_ref[-2 * share :, :]) + merge(down_ref[-2 * share :, :]))
    for copy in range(copies_ref.shape[0]):
        copies_ref[copy] = total
    copies.append(pltpu.make_async_copy(copies_ref, out_ref, sems.at[2]))
    copies[-1].start()
    for copy in copies:
        copy.wait()


def finish(parts, rows, places, near, total, replicas, rows_shape):
    share = total.shape[0]
    shape = (replicas,) + total.shape
    return pl.pallas_call(
        functools.partial(finish_kernel, rows, places, share),
        out_shape=(
            pltpu.HBM(near.shape, near.dtype),
            pltpu.HBM(shape, jnp.float32),
            pltpu.VMEM(rows_shape, jnp.bfloat16),
        ),
        in_specs=[VECTOR, VECTOR, OUTER, VECTOR],
        out_specs=(OUTER, OUTER, VECTOR),
        scratch_shapes=[pltpu.VMEM(shape, jnp.float32), pltpu.SemaphoreType.DMA((3,))],
        input_output_aliases={2: 0},
        compiler_params=pltpu.CompilerParams(vmem_limit_bytes=4 * MIB),
        name="finish",
    )(*parts, outer(near), total)


def on_device(user_factors, item_factors, tile_users, tile_counts):
    chips = lax.axis_size("grp") // CORES
    replicas = lax.axis_size("rep")
    owned_rows, features = user_factors.shape
    blocks = item_factors.shape[0] // IBLK
    share = features // replicas
    parts = 2 * share
    shift = functools.partial(chip_shift, chips=chips)
    bar = lax.optimization_barrier

    def half_rows(count):
        return jax.ShapeDtypeStruct((count, features), jnp.bfloat16)

    square = jax.ShapeDtypeStruct((features, features), jnp.float32)
    gram, own = small_call(gram_kernel, (square, half_rows(owned_rows)), "local_gram", user_factors)
    pieces = lax.all_to_all(gram, "rep", 0, 0, tiled=True)
    gram = jnp.sum(pieces.reshape(replicas, share, features), axis=0)
    own = small_call(own_kernel, half_rows(owned_rows + parts), "own", own, gram, core_swap(gram, chips))

    below, above = shift(own, distance=STRIDE), shift(own, distance=-STRIDE)
    far_below, far_above = shift(below, distance=STRIDE), shift(above, distance=-STRIDE)
    weight = small_call(
        weight_kernel,
        pltpu.VMEM((blocks, IBLK, tile_counts.shape[0] * UROWS // blocks), jnp.bfloat16),
        "item_weights",
        tile_counts,
    )
    far_above, weight = bar((far_above, weight))
    up, down = small_call(
        functools.partial(pack_kernel, owned_rows),
        (half_rows(5 * owned_rows + parts), half_rows(4 * owned_rows + parts)),
        "pack",
        own,
        below,
        above,
        far_below,
        far_above,
    )
    up_rows, down_rows = 5 * owned_rows, 4 * owned_rows
    near_shape = pltpu.HBM((chips * owned_rows, features), jnp.bfloat16)
    near, total = collect("collect_0", [up], [up_rows], [0], near_shape, share)
    places = pool_places(tile_users, chips, replicas, owned_rows // UROWS)
    for hop in range(1, HOPS + 1):
        up, down = shift(up, distance=1), shift(down, distance=-1)
        down, near, total, places = bar((down, near, total, places))
        at = [hop * up_rows, (HOPS + 1) * up_rows + (hop - 1) * down_rows]
        if hop < HOPS:
            name = "collect_" + str(hop)
            near, total = collect(name, [up, down], [up_rows, down_rows], at, near_shape, share, near, total)

    rows_shape = (tile_counts.shape[0] * UROWS, features)
    near, copies, rows = finish([up, down], [up_rows, down_rows], at, near, total, replicas, rows_shape)
    other = core_swap(near, chips)
    gram = lax.all_to_all(copies.reshape(features, features), "rep", 0, 0, tiled=True)
    rows, started = first_residue(places, near, other, weight, item_factors, rows)
    return solve_steps(rows, weight, item_factors, started, gram)


def solution(mesh):
    in_specs = (
        P(("grp", "rep"), None),
        P(("grp", "rep"), None),
        P(("grp", "rep")),
        P(("grp", "rep"), None, None),
    )
    out_specs = P(("grp", "rep"), None)
    return jax.shard_map(
        on_device, mesh=mesh, in_specs=in_specs, out_specs=out_specs, check_vma=False
    )
```

```python
import functools

import jax
import jax.numpy as jnp
import numpy as np
from jax import lax
from jax.experimental import pallas as pl
from jax.experimental.pallas import tpu as pltpu
from jax.sharding import PartitionSpec as P

UROWS = 64
IBLK = 128
ITERS = 3
CORES = 2
HOPS = 3
STRIDE = 2 * HOPS + 1
CHUNK = 256
MIB = 1024 * 1024

ALPHA = 8.0
LAMBDA = 1.0
EPSILON = 1e-06


def chip_shift(value, chips, distance):
    pairs = [
        (CORES * chip + core, CORES * ((chip + (1 - 2 * core) * distance) % chips) + core)
        for chip in range(chips)
        for core in range(CORES)
    ]
    return lax.ppermute(value, "grp", pairs)


def core_swap(value, chips):
    pairs = [(CORES * chip + core, CORES * chip + 1 - core) for chip in range(chips) for core in range(CORES)]
    return lax.ppermute(value, "grp", pairs)


def slot_table(chips):
    slots = [0, -STRIDE, STRIDE, -2 * STRIDE, 2 * STRIDE]
    order = [slot - hop for hop in range(HOPS + 1) for slot in slots]
    order += [slot + hop for hop in range(1, HOPS + 1) for slot in slots[:-1]]
    table = np.full((chips,), -1, np.int32)
    for place, distance in enumerate(order):
        table[distance % chips] = place
    assert len(order) == chips and (table >= 0).all()
    return table


def pool_places(tile_users, chips, replicas, owned):
    member = tile_users // (owned * replicas)
    core = member % CORES
    here = lax.axis_index("grp")
    ahead = ((1 - 2 * core) * (member // CORES - here // CORES) + chips) % chips
    distances = np.arange(chips, dtype=np.int32)
    slot = jnp.sum(jnp.where(ahead[:, None] == distances, slot_table(chips), 0), axis=1)
    other_core = (core != here % CORES).astype(jnp.int32)
    return ((other_core * chips + slot) * owned + tile_users % owned).astype(jnp.int32)


def merge(parts):
    half = parts.shape[0] // 2
    return parts[:half].astype(jnp.float32) + parts[half:].astype(jnp.float32)


def dot(left, right):
    return jnp.dot(left, right, preferred_element_type=jnp.float32)


def dot_turned(left, right):
    return lax.dot_general(left, right, (((1,), (1,)), ((), ())), preferred_element_type=jnp.float32)


def high_low(value):
    high = value.astype(jnp.bfloat16)
    return high, (value - high.astype(jnp.float32)).astype(jnp.bfloat16)


def item_rows(block):
    return slice(block * IBLK, (block + 1) * IBLK)


SCALAR = pl.BlockSpec(memory_space=pltpu.SMEM)
VECTOR = pl.BlockSpec(memory_space=pltpu.VMEM)
OUTER = pl.BlockSpec(memory_space=pltpu.HBM)


def outer(value):
    return pltpu.with_memory_space_constraint(value, pltpu.HBM)


def inner(value):
    return pltpu.with_memory_space_constraint(value, pltpu.VMEM)


def small_call(kernel, outs, name, *args):
    return pl.pallas_call(
        kernel,
        out_shape=outs,
        in_specs=[VECTOR] * len(args),
        out_specs=jax.tree.map(lambda _: VECTOR, outs),
        compiler_params=pltpu.CompilerParams(vmem_limit_bytes=8 * MIB),
        name=name,
    )(*args)


def gram_kernel(users_ref, gram_ref, own_ref):
    high, low = high_low(users_ref[...])
    own_ref[...] = high
    dims = (((0,), (0,)), ((), ()))
    product = functools.partial(lax.dot_general, dimension_numbers=dims, preferred_element_type=jnp.float32)
    gram_ref[...] = product(high, high) + (product(high, low) + product(low, high))


def weight_kernel(counts_ref, weight_ref):
    blocks, _, depth = weight_ref.shape
    tiles = IBLK // UROWS
    for block in range(blocks):
        for start in range(0, depth, IBLK):
            first = (block * depth + start) // UROWS
            counts = counts_ref[first : first + tiles].reshape(IBLK, IBLK).astype(jnp.float32)
            weight_ref[block, :, start : start + IBLK] = (ALPHA * counts).T.astype(jnp.bfloat16)


def tile_part(total, high, block, rows_ref, weight_ref):
    depth = weight_ref.shape[2]
    for start in range(0, depth, CHUNK):
        rows = rows_ref[block * depth + start : block * depth + start + CHUNK, :]
        scores = dot_turned(high, rows)
        weight = weight_ref[block, :, start : start + CHUNK].astype(jnp.float32)
        total = total + dot((weight * scores).astype(jnp.bfloat16), rows)
    return total


def first_kernel(
    places_ref, near_ref, other_ref, weight_ref, items_in_ref, open_rows_ref, rows_ref, started_out_ref, items_ref,
    started_ref, items_sem, sems, started_sems,
):
    del open_rows_ref
    near_blocks = near_ref.shape[0] // UROWS
    blocks, _, depth = weight_ref.shape
    per_block = depth // UROWS
    bring_items = pltpu.make_async_copy(items_in_ref, items_ref, items_sem)
    bring_items.start()

    def fetch(tile, block):
        place = places_ref[tile]
        to = rows_ref.at[pl.ds(pl.multiple_of(tile * UROWS, UROWS), UROWS), :]

        @pl.when(place < near_blocks)
        def _():
            at = pl.ds(pl.multiple_of(place * UROWS, UROWS), UROWS)
            pltpu.make_async_copy(near_ref.at[at, :], to, sems.at[block]).start()

        @pl.when(place >= near_blocks)
        def _():
            at = pl.ds(pl.multiple_of((place - near_blocks) * UROWS, UROWS), UROWS)
            pltpu.make_async_copy(other_ref.at[at, :], to, sems.at[block]).start()

        return block

    for block in range(blocks):
        lax.fori_loop(block * per_block, (block + 1) * per_block, fetch, block)
    bring_items.wait()
    kept = []
    for block in range(blocks):
        mine = rows_ref.at[block * depth : (block + 1) * depth, :]
        pltpu.make_async_copy(mine, mine, sems.at[block]).wait()
        guess = items_ref[item_rows(block), :]
        target = -LAMBDA * guess
        for start in range(0, depth, CHUNK):
            weight = weight_ref[block, :, start : start + CHUNK]
            confidence = weight + jnp.where(weight > 0, 1.0, 0.0).astype(jnp.bfloat16)
            target = target + dot(confidence, rows_ref[block * depth + start : block * depth + start + CHUNK, :])
        part = tile_part(jnp.zeros_like(guess), guess.astype(jnp.bfloat16), block, rows_ref, weight_ref)
        started_ref[item_rows(block), :] = target - part
        span = item_rows(block)
        kept.append(
            pltpu.make_async_copy(started_ref.at[span, :], started_out_ref.at[span, :], started_sems.at[block])
        )
        kept[-1].start()
    for copy in kept:
        copy.wait()


def first_residue(places, near, other, weight, items, rows):
    blocks = weight.shape[0]
    return pl.pallas_call(
        first_kernel,
        out_shape=(pltpu.VMEM(rows.shape, rows.dtype), pltpu.HBM(items.shape, jnp.float32)),
        in_specs=[SCALAR, OUTER, pl.BlockSpec(memory_space=pl.ANY), VECTOR, OUTER, VECTOR],
        out_specs=(VECTOR, OUTER),
        scratch_shapes=[
            pltpu.VMEM(items.shape, jnp.float32),
            pltpu.VMEM(items.shape, jnp.float32),
            pltpu.SemaphoreType.DMA,
            pltpu.SemaphoreType.DMA((blocks,)),
            pltpu.SemaphoreType.DMA((blocks,)),
        ],
        compiler_params=pltpu.CompilerParams(vmem_limit_bytes=8 * MIB),
        input_output_aliases={5: 0},
        name="first_residue",
    )(places, outer(near), other, inner(weight), outer(items), inner(rows))


def steps_kernel(
    rows_ref, weight_ref, items_ref, started_ref, gram_ref, guess_ref, high_ref, low_ref, residue_ref, direction_ref,
    applied_ref, sems,
):
    bring_items = pltpu.make_async_copy(items_ref, guess_ref, sems.at[0])
    bring_items.start()
    bring_started = pltpu.make_async_copy(started_ref, residue_ref, sems.at[1])
    bring_started.start()
    blocks = weight_ref.shape[0]
    high_ref[...], low_ref[...] = high_low(gram_ref[...])

    def gram_part(vector):
        high, low = high_low(vector)
        return dot(high, high_ref[...]) + (dot(high, low_ref[...]) + dot(low, high_ref[...]))

    bring_items.wait()
    first = gram_part(guess_ref[...])
    bring_started.wait()
    residue = residue_ref[...] - first
    residue_ref[...] = residue
    direction_ref[...] = residue

    def step(iteration, current):
        vector = direction_ref[...]
        applied_ref[...] = vector * LAMBDA + gram_part(vector)
        for block in range(blocks):
            span = item_rows(block)
            high = direction_ref[span, :].astype(jnp.bfloat16)
            applied_ref[span, :] = tile_part(applied_ref[span, :], high, block, rows_ref, weight_ref)
        direction = direction_ref[...]
        applied = applied_ref[...]
        size = current / (jnp.sum(direction * applied, axis=1, keepdims=True) + EPSILON)
        guess_ref[...] += size * direction
        residue = residue_ref[...] - size * applied
        residue_ref[...] = residue
        following = jnp.sum(residue * residue, axis=1, keepdims=True)
        direction_ref[...] = residue + (following / (current + EPSILON)) * direction
        return following

    lax.fori_loop(0, ITERS, step, jnp.sum(residue * residue, axis=1, keepdims=True))


def solve_steps(rows, weight, items, started, gram):
    features = items.shape[1]
    state = pltpu.VMEM(items.shape, jnp.float32)
    square = pltpu.VMEM((features, features), jnp.bfloat16)
    return pl.pallas_call(
        steps_kernel,
        out_shape=jax.ShapeDtypeStruct(items.shape, jnp.float32),
        in_specs=[VECTOR, VECTOR, OUTER, OUTER, VECTOR],
        out_specs=VECTOR,
        scratch_shapes=[square, square, state, state, state, pltpu.SemaphoreType.DMA((2,))],
        compiler_params=pltpu.CompilerParams(vmem_limit_bytes=10 * MIB),
        name="solve_steps",
    )(inner(rows), inner(weight), outer(items), outer(started), gram)


def put_parts(ref, start, value):
    count = value.shape[0]
    ref[start : start + count, :], ref[start + count : start + 2 * count, :] = high_low(value)


def own_kernel(own_ref, gram_ref, out_ref):
    rows = own_ref.shape[0]
    out_ref[:rows, :] = own_ref[...]
    put_parts(out_ref, rows, gram_ref[...])


def pair_kernel(mine_ref, other_ref, out_ref):
    rows = out_ref.shape[0] - mine_ref.shape[0]
    out_ref[:rows, :] = mine_ref[:rows, :]
    out_ref[rows : 2 * rows, :] = other_ref[:rows, :]
    put_parts(out_ref, 2 * rows, merge(mine_ref[rows:, :]) + merge(other_ref[rows:, :]))


def pack_kernel(rows, *refs):
    parts, (up_ref, down_ref) = refs[:-2], refs[-2:]
    parts_rows = up_ref.shape[0] - len(parts) * rows
    total = None
    for place, part in enumerate(parts):
        up_ref[place * rows : (place + 1) * rows, :] = part[:rows, :]
        if place < len(parts) - 1:
            down_ref[place * rows : (place + 1) * rows, :] = part[:rows, :]
        else:
            put_parts(down_ref, place * rows, total)
        piece = merge(part[-parts_rows:, :])
        total = piece if total is None else total + piece
    put_parts(up_ref, len(parts) * rows, total)


def collect_kernel(rows, places, share, *refs):
    parts, (near_ref, total_ref, sems) = refs[: len(rows)], refs[-3:]
    copies = []
    for at, part in enumerate(parts):
        to = near_ref.at[places[at] : places[at] + rows[at], :]
        copies.append(pltpu.make_async_copy(part.at[: rows[at], :], to, sems.at[at]))
        copies[-1].start()
    total = functools.reduce(jnp.add, [merge(part[-2 * share :, :]) for part in parts])
    total_ref[...] = total if len(refs) == len(rows) + 3 else refs[len(rows) + 1][...] + total
    for copy in copies:
        copy.wait()


def collect(name, parts, rows, places, near_shape, share, *earlier):
    count = len(parts)
    return pl.pallas_call(
        functools.partial(collect_kernel, rows, places, share),
        out_shape=(near_shape, jax.ShapeDtypeStruct((share, near_shape.shape[1]), jnp.float32)),
        in_specs=[VECTOR] * count + [OUTER, VECTOR][: len(earlier)],
        out_specs=(OUTER, VECTOR),
        scratch_shapes=[pltpu.SemaphoreType.DMA((count,))],
        input_output_aliases={count: 0} if earlier else {},
        compiler_params=pltpu.CompilerParams(vmem_limit_bytes=4 * MIB),
        name=name,
    )(*parts, *map(outer, earlier[:1]), *earlier[1:])


def finish_kernel(rows, places, share, up_ref, down_ref, near_in_ref, total_ref, near_ref, out_ref, rows_ref, copies_ref, sems):
    del near_in_ref, rows_ref
    copies = []
    for at, part in enumerate((up_ref, down_ref)):
        to = near_ref.at[places[at] : places[at] + rows[at], :]
        copies.append(pltpu.make_async_copy(part.at[: rows[at], :], to, sems.at[at]))
        copies[-1].start()
    total = total_ref[...] + (merge(up_ref[-2 * share :, :]) + merge(down_ref[-2 * share :, :]))
    for copy in range(copies_ref.shape[0]):
        copies_ref[copy] = total
    copies.append(pltpu.make_async_copy(copies_ref, out_ref, sems.at[2]))
    copies[-1].start()
    for copy in copies:
        copy.wait()


def finish(parts, rows, places, near, total, replicas, rows_shape):
    share = total.shape[0]
    shape = (replicas,) + total.shape
    return pl.pallas_call(
        functools.partial(finish_kernel, rows, places, share),
        out_shape=(
            pltpu.HBM(near.shape, near.dtype),
            pltpu.HBM(shape, jnp.float32),
            pltpu.VMEM(rows_shape, jnp.bfloat16),
        ),
        in_specs=[VECTOR, VECTOR, OUTER, VECTOR],
        out_specs=(OUTER, OUTER, VECTOR),
        scratch_shapes=[pltpu.VMEM(shape, jnp.float32), pltpu.SemaphoreType.DMA((3,))],
        input_output_aliases={2: 0},
        compiler_params=pltpu.CompilerParams(vmem_limit_bytes=4 * MIB),
        name="finish",
    )(*parts, outer(near), total)


def on_device(user_factors, item_factors, tile_users, tile_counts):
    chips = lax.axis_size("grp") // CORES
    replicas = lax.axis_size("rep")
    owned_rows, features = user_factors.shape
    blocks = item_factors.shape[0] // IBLK
    share = features // replicas
    parts = 2 * share
    shift = functools.partial(chip_shift, chips=chips)
    bar = lax.optimization_barrier

    def half_rows(count):
        return jax.ShapeDtypeStruct((count, features), jnp.bfloat16)

    square = jax.ShapeDtypeStruct((features, features), jnp.float32)
    gram, own = small_call(gram_kernel, (square, half_rows(owned_rows)), "local_gram", user_factors)
    pieces = lax.all_to_all(gram, "rep", 0, 0, tiled=True)
    gram = jnp.sum(pieces.reshape(replicas, share, features), axis=0)
    mine = small_call(own_kernel, half_rows(owned_rows + parts), "own", own, gram)
    own = small_call(pair_kernel, half_rows(2 * owned_rows + parts), "pair", mine, core_swap(mine, chips))

    below = shift(own, distance=STRIDE)
    far_below = shift(below, distance=STRIDE)
    above = core_swap(below[owned_rows:], chips)
    weight = small_call(
        weight_kernel,
        pltpu.VMEM((blocks, IBLK, tile_counts.shape[0] * UROWS // blocks), jnp.bfloat16),
        "item_weights",
        tile_counts,
    )
    far_below, above, weight = bar((far_below, above, weight))
    far_above = core_swap(far_below[owned_rows:], chips)
    up, down = small_call(
        functools.partial(pack_kernel, owned_rows),
        (half_rows(5 * owned_rows + parts), half_rows(4 * owned_rows + parts)),
        "pack",
        own,
        below,
        above,
        far_below,
        far_above,
    )
    up_rows, down_rows = 5 * owned_rows, 4 * owned_rows
    near_shape = pltpu.HBM((chips * owned_rows, features), jnp.bfloat16)
    near, total = collect("collect_0", [up], [up_rows], [0], near_shape, share)
    places = pool_places(tile_users, chips, replicas, owned_rows // UROWS)
    for hop in range(1, HOPS + 1):
        up, down = shift(up, distance=1), shift(down, distance=-1)
        down, near, total, places = bar((down, near, total, places))
        at = [hop * up_rows, (HOPS + 1) * up_rows + (hop - 1) * down_rows]
        if hop < HOPS:
            name = "collect_" + str(hop)
            near, total = collect(name, [up, down], [up_rows, down_rows], at, near_shape, share, near, total)

    rows_shape = (tile_counts.shape[0] * UROWS, features)
    near, copies, rows = finish([up, down], [up_rows, down_rows], at, near, total, replicas, rows_shape)
    other = core_swap(near, chips)
    gram = lax.all_to_all(copies.reshape(features, features), "rep", 0, 0, tiled=True)
    rows, started = first_residue(places, near, other, weight, item_factors, rows)
    return solve_steps(rows, weight, item_factors, started, gram)


def solution(mesh):
    in_specs = (
        P(("grp", "rep"), None),
        P(("grp", "rep"), None),
        P(("grp", "rep")),
        P(("grp", "rep"), None, None),
    )
    out_specs = P(("grp", "rep"), None)
    return jax.shard_map(
        on_device, mesh=mesh, in_specs=in_specs, out_specs=out_specs, check_vma=False
    )
```

```python
import functools

import jax
import jax.numpy as jnp
import numpy as np
from jax import lax
from jax.experimental import pallas as pl
from jax.experimental.pallas import tpu as pltpu
from jax.sharding import PartitionSpec as P

UROWS = 64
IBLK = 128
ITERS = 3
CORES = 2
HOPS = 3
STRIDE = 2 * HOPS + 1
CHUNK = 256
MIB = 1024 * 1024

ALPHA = 8.0
LAMBDA = 1.0
EPSILON = 1e-06


def chip_shift(value, chips, distance):
    pairs = [
        (CORES * chip + core, CORES * ((chip + (1 - 2 * core) * distance) % chips) + core)
        for chip in range(chips)
        for core in range(CORES)
    ]
    return lax.ppermute(value, "grp", pairs)


def core_swap(value, chips):
    pairs = [(CORES * chip + core, CORES * chip + 1 - core) for chip in range(chips) for core in range(CORES)]
    return lax.ppermute(value, "grp", pairs)


def slot_table(chips):
    slots = [0, -STRIDE, STRIDE, -2 * STRIDE, 2 * STRIDE]
    order = [slot - hop for hop in range(HOPS + 1) for slot in slots]
    order += [slot + hop for hop in range(1, HOPS + 1) for slot in slots[:-1]]
    table = np.full((chips,), -1, np.int32)
    for place, distance in enumerate(order):
        table[distance % chips] = place
    assert len(order) == chips and (table >= 0).all()
    return table


def pool_places(tile_users, chips, replicas, owned):
    member = tile_users // (owned * replicas)
    core = member % CORES
    here = lax.axis_index("grp")
    ahead = ((1 - 2 * core) * (member // CORES - here // CORES) + chips) % chips
    distances = np.arange(chips, dtype=np.int32)
    slot = jnp.sum(jnp.where(ahead[:, None] == distances, slot_table(chips), 0), axis=1)
    other_core = (core != here % CORES).astype(jnp.int32)
    return ((other_core * chips + slot) * owned + tile_users % owned).astype(jnp.int32)


def merge(parts):
    half = parts.shape[0] // 2
    return parts[:half].astype(jnp.float32) + parts[half:].astype(jnp.float32)


def dot(left, right):
    return jnp.dot(left, right, preferred_element_type=jnp.float32)


def dot_turned(left, right):
    return lax.dot_general(left, right, (((1,), (1,)), ((), ())), preferred_element_type=jnp.float32)


def high_low(value):
    high = value.astype(jnp.bfloat16)
    return high, (value - high.astype(jnp.float32)).astype(jnp.bfloat16)


def item_rows(block):
    return slice(block * IBLK, (block + 1) * IBLK)


SCALAR = pl.BlockSpec(memory_space=pltpu.SMEM)
VECTOR = pl.BlockSpec(memory_space=pltpu.VMEM)
OUTER = pl.BlockSpec(memory_space=pltpu.HBM)


def outer(value):
    return pltpu.with_memory_space_constraint(value, pltpu.HBM)


def inner(value):
    return pltpu.with_memory_space_constraint(value, pltpu.VMEM)


def small_call(kernel, outs, name, *args):
    return pl.pallas_call(
        kernel,
        out_shape=outs,
        in_specs=[VECTOR] * len(args),
        out_specs=jax.tree.map(lambda _: VECTOR, outs),
        compiler_params=pltpu.CompilerParams(vmem_limit_bytes=8 * MIB),
        name=name,
    )(*args)


def gram_kernel(users_ref, gram_ref, own_ref):
    high, low = high_low(users_ref[...])
    own_ref[...] = high
    dims = (((0,), (0,)), ((), ()))
    product = functools.partial(lax.dot_general, dimension_numbers=dims, preferred_element_type=jnp.float32)
    gram_ref[...] = product(high, high) + (product(high, low) + product(low, high))


def weight_kernel(counts_ref, weight_ref):
    blocks, _, depth = weight_ref.shape
    tiles = IBLK // UROWS
    for block in range(blocks):
        for start in range(0, depth, IBLK):
            first = (block * depth + start) // UROWS
            counts = counts_ref[first : first + tiles].reshape(IBLK, IBLK).astype(jnp.float32)
            weight_ref[block, :, start : start + IBLK] = (ALPHA * counts).T.astype(jnp.bfloat16)


def tile_part(total, high, block, rows_ref, weight_ref):
    depth = weight_ref.shape[2]
    for start in range(0, depth, CHUNK):
        rows = rows_ref[block * depth + start : block * depth + start + CHUNK, :]
        scores = dot_turned(high, rows)
        weight = weight_ref[block, :, start : start + CHUNK].astype(jnp.float32)
        total = total + dot((weight * scores).astype(jnp.bfloat16), rows)
    return total


def first_kernel(
    places_ref, near_ref, other_ref, weight_ref, items_in_ref, open_rows_ref, rows_ref, started_out_ref, items_ref,
    started_ref, items_sem, sems, started_sems,
):
    del open_rows_ref
    near_blocks = near_ref.shape[0] // UROWS
    blocks, _, depth = weight_ref.shape
    per_block = depth // UROWS
    bring_items = pltpu.make_async_copy(items_in_ref, items_ref, items_sem)
    bring_items.start()

    def fetch(tile, block):
        place = places_ref[tile]
        to = rows_ref.at[pl.ds(pl.multiple_of(tile * UROWS, UROWS), UROWS), :]

        @pl.when(place < near_blocks)
        def _():
            at = pl.ds(pl.multiple_of(place * UROWS, UROWS), UROWS)
            pltpu.make_async_copy(near_ref.at[at, :], to, sems.at[block]).start()

        @pl.when(place >= near_blocks)
        def _():
            at = pl.ds(pl.multiple_of((place - near_blocks) * UROWS, UROWS), UROWS)
            pltpu.make_async_copy(other_ref.at[at, :], to, sems.at[block]).start()

        return block

    for block in range(blocks):
        lax.fori_loop(block * per_block, (block + 1) * per_block, fetch, block)
    bring_items.wait()
    kept = []
    for block in range(blocks):
        mine = rows_ref.at[block * depth : (block + 1) * depth, :]
        pltpu.make_async_copy(mine, mine, sems.at[block]).wait()
        guess = items_ref[item_rows(block), :]
        target = -LAMBDA * guess
        for start in range(0, depth, CHUNK):
            weight = weight_ref[block, :, start : start + CHUNK]
            confidence = weight + jnp.where(weight > 0, 1.0, 0.0).astype(jnp.bfloat16)
            target = target + dot(confidence, rows_ref[block * depth + start : block * depth + start + CHUNK, :])
        part = tile_part(jnp.zeros_like(guess), guess.astype(jnp.bfloat16), block, rows_ref, weight_ref)
        started_ref[item_rows(block), :] = target - part
        span = item_rows(block)
        kept.append(
            pltpu.make_async_copy(started_ref.at[span, :], started_out_ref.at[span, :], started_sems.at[block])
        )
        kept[-1].start()
    for copy in kept:
        copy.wait()


def first_residue(places, near, other, weight, items, rows):
    blocks = weight.shape[0]
    return pl.pallas_call(
        first_kernel,
        out_shape=(pltpu.VMEM(rows.shape, rows.dtype), pltpu.HBM(items.shape, jnp.float32)),
        in_specs=[SCALAR, OUTER, pl.BlockSpec(memory_space=pl.ANY), VECTOR, OUTER, VECTOR],
        out_specs=(VECTOR, OUTER),
        scratch_shapes=[
            pltpu.VMEM(items.shape, jnp.float32),
            pltpu.VMEM(items.shape, jnp.float32),
            pltpu.SemaphoreType.DMA,
            pltpu.SemaphoreType.DMA((blocks,)),
            pltpu.SemaphoreType.DMA((blocks,)),
        ],
        compiler_params=pltpu.CompilerParams(vmem_limit_bytes=8 * MIB),
        input_output_aliases={5: 0},
        name="first_residue",
    )(places, outer(near), other, inner(weight), outer(items), inner(rows))


def steps_kernel(
    rows_ref, weight_ref, items_ref, started_ref, gram_ref, guess_ref, high_ref, low_ref, residue_ref, direction_ref,
    applied_ref, sems,
):
    bring_items = pltpu.make_async_copy(items_ref, guess_ref, sems.at[0])
    bring_items.start()
    bring_started = pltpu.make_async_copy(started_ref, residue_ref, sems.at[1])
    bring_started.start()
    blocks = weight_ref.shape[0]
    high_ref[...], low_ref[...] = high_low(gram_ref[...])

    def gram_part(vector):
        high, low = high_low(vector)
        return dot(high, high_ref[...]) + (dot(high, low_ref[...]) + dot(low, high_ref[...]))

    bring_items.wait()
    first = gram_part(guess_ref[...])
    bring_started.wait()
    residue = residue_ref[...] - first
    residue_ref[...] = residue
    direction_ref[...] = residue

    def operate():
        vector = direction_ref[...]
        applied_ref[...] = vector * LAMBDA + gram_part(vector)
        for block in range(blocks):
            span = item_rows(block)
            high = direction_ref[span, :].astype(jnp.bfloat16)
            applied_ref[span, :] = tile_part(applied_ref[span, :], high, block, rows_ref, weight_ref)

    def step_size(current):
        return current / (jnp.sum(direction_ref[...] * applied_ref[...], axis=1, keepdims=True) + EPSILON)

    def step(iteration, current):
        operate()
        size = step_size(current)
        direction = direction_ref[...]
        guess_ref[...] += size * direction
        residue = residue_ref[...] - size * applied_ref[...]
        residue_ref[...] = residue
        following = jnp.sum(residue * residue, axis=1, keepdims=True)
        direction_ref[...] = residue + (following / (current + EPSILON)) * direction
        return following

    current = lax.fori_loop(0, ITERS - 1, step, jnp.sum(residue * residue, axis=1, keepdims=True))
    operate()
    guess_ref[...] += step_size(current) * direction_ref[...]


def solve_steps(rows, weight, items, started, gram):
    features = items.shape[1]
    state = pltpu.VMEM(items.shape, jnp.float32)
    square = pltpu.VMEM((features, features), jnp.bfloat16)
    return pl.pallas_call(
        steps_kernel,
        out_shape=jax.ShapeDtypeStruct(items.shape, jnp.float32),
        in_specs=[VECTOR, VECTOR, OUTER, OUTER, VECTOR],
        out_specs=VECTOR,
        scratch_shapes=[square, square, state, state, state, pltpu.SemaphoreType.DMA((2,))],
        compiler_params=pltpu.CompilerParams(vmem_limit_bytes=10 * MIB),
        name="solve_steps",
    )(inner(rows), inner(weight), outer(items), outer(started), gram)


def put_parts(ref, start, value):
    count = value.shape[0]
    ref[start : start + count, :], ref[start + count : start + 2 * count, :] = high_low(value)


def own_kernel(own_ref, gram_ref, out_ref):
    rows = own_ref.shape[0]
    out_ref[:rows, :] = own_ref[...]
    put_parts(out_ref, rows, gram_ref[...])


def pair_kernel(mine_ref, other_ref, out_ref):
    rows = out_ref.shape[0] - mine_ref.shape[0]
    out_ref[:rows, :] = mine_ref[:rows, :]
    out_ref[rows : 2 * rows, :] = other_ref[:rows, :]
    put_parts(out_ref, 2 * rows, merge(mine_ref[rows:, :]) + merge(other_ref[rows:, :]))


def pack_kernel(rows, *refs):
    parts, (up_ref, down_ref) = refs[:-2], refs[-2:]
    parts_rows = up_ref.shape[0] - len(parts) * rows
    total = None
    for place, part in enumerate(parts):
        up_ref[place * rows : (place + 1) * rows, :] = part[:rows, :]
        if place < len(parts) - 1:
            down_ref[place * rows : (place + 1) * rows, :] = part[:rows, :]
        else:
            put_parts(down_ref, place * rows, total)
        piece = merge(part[-parts_rows:, :])
        total = piece if total is None else total + piece
    put_parts(up_ref, len(parts) * rows, total)


def collect_kernel(rows, places, share, *refs):
    parts, (near_ref, total_ref, sems) = refs[: len(rows)], refs[-3:]
    copies = []
    for at, part in enumerate(parts):
        to = near_ref.at[places[at] : places[at] + rows[at], :]
        copies.append(pltpu.make_async_copy(part.at[: rows[at], :], to, sems.at[at]))
        copies[-1].start()
    total = functools.reduce(jnp.add, [merge(part[-2 * share :, :]) for part in parts])
    total_ref[...] = total if len(refs) == len(rows) + 3 else refs[len(rows) + 1][...] + total
    for copy in copies:
        copy.wait()


def collect(name, parts, rows, places, near_shape, share, *earlier):
    count = len(parts)
    return pl.pallas_call(
        functools.partial(collect_kernel, rows, places, share),
        out_shape=(near_shape, jax.ShapeDtypeStruct((share, near_shape.shape[1]), jnp.float32)),
        in_specs=[VECTOR] * count + [OUTER, VECTOR][: len(earlier)],
        out_specs=(OUTER, VECTOR),
        scratch_shapes=[pltpu.SemaphoreType.DMA((count,))],
        input_output_aliases={count: 0} if earlier else {},
        compiler_params=pltpu.CompilerParams(vmem_limit_bytes=4 * MIB),
        name=name,
    )(*parts, *map(outer, earlier[:1]), *earlier[1:])


def finish_kernel(rows, places, share, up_ref, down_ref, near_in_ref, total_ref, near_ref, out_ref, rows_ref, copies_ref, sems):
    del near_in_ref, rows_ref
    copies = []
    for at, part in enumerate((up_ref, down_ref)):
        to = near_ref.at[places[at] : places[at] + rows[at], :]
        copies.append(pltpu.make_async_copy(part.at[: rows[at], :], to, sems.at[at]))
        copies[-1].start()
    total = total_ref[...] + (merge(up_ref[-2 * share :, :]) + merge(down_ref[-2 * share :, :]))
    for copy in range(copies_ref.shape[0]):
        copies_ref[copy] = total
    copies.append(pltpu.make_async_copy(copies_ref, out_ref, sems.at[2]))
    copies[-1].start()
    for copy in copies:
        copy.wait()


def finish(parts, rows, places, near, total, replicas, rows_shape):
    share = total.shape[0]
    shape = (replicas,) + total.shape
    return pl.pallas_call(
        functools.partial(finish_kernel, rows, places, share),
        out_shape=(
            pltpu.HBM(near.shape, near.dtype),
            pltpu.HBM(shape, jnp.float32),
            pltpu.VMEM(rows_shape, jnp.bfloat16),
        ),
        in_specs=[VECTOR, VECTOR, OUTER, VECTOR],
        out_specs=(OUTER, OUTER, VECTOR),
        scratch_shapes=[pltpu.VMEM(shape, jnp.float32), pltpu.SemaphoreType.DMA((3,))],
        input_output_aliases={2: 0},
        compiler_params=pltpu.CompilerParams(vmem_limit_bytes=4 * MIB),
        name="finish",
    )(*parts, outer(near), total)


def on_device(user_factors, item_factors, tile_users, tile_counts):
    chips = lax.axis_size("grp") // CORES
    replicas = lax.axis_size("rep")
    owned_rows, features = user_factors.shape
    blocks = item_factors.shape[0] // IBLK
    share = features // replicas
    parts = 2 * share
    shift = functools.partial(chip_shift, chips=chips)
    bar = lax.optimization_barrier

    def half_rows(count):
        return jax.ShapeDtypeStruct((count, features), jnp.bfloat16)

    square = jax.ShapeDtypeStruct((features, features), jnp.float32)
    gram, own = small_call(gram_kernel, (square, half_rows(owned_rows)), "local_gram", user_factors)
    pieces = lax.all_to_all(gram, "rep", 0, 0, tiled=True)
    gram = jnp.sum(pieces.reshape(replicas, share, features), axis=0)
    mine = small_call(own_kernel, half_rows(owned_rows + parts), "own", own, gram)
    own = small_call(pair_kernel, half_rows(2 * owned_rows + parts), "pair", mine, core_swap(mine, chips))

    below = shift(own, distance=STRIDE)
    far_below = shift(below, distance=STRIDE)
    above = core_swap(below[owned_rows:], chips)
    weight = small_call(
        weight_kernel,
        pltpu.VMEM((blocks, IBLK, tile_counts.shape[0] * UROWS // blocks), jnp.bfloat16),
        "item_weights",
        tile_counts,
    )
    far_below, above, weight = bar((far_below, above, weight))
    far_above = core_swap(far_below[owned_rows:], chips)
    up, down = small_call(
        functools.partial(pack_kernel, owned_rows),
        (half_rows(5 * owned_rows + parts), half_rows(4 * owned_rows + parts)),
        "pack",
        own,
        below,
        above,
        far_below,
        far_above,
    )
    up_rows, down_rows = 5 * owned_rows, 4 * owned_rows
    near_shape = pltpu.HBM((chips * owned_rows, features), jnp.bfloat16)
    near, total = collect("collect_0", [up], [up_rows], [0], near_shape, share)
    places = pool_places(tile_users, chips, replicas, owned_rows // UROWS)
    for hop in range(1, HOPS + 1):
        up, down = shift(up, distance=1), shift(down, distance=-1)
        down, near, total, places = bar((down, near, total, places))
        at = [hop * up_rows, (HOPS + 1) * up_rows + (hop - 1) * down_rows]
        if hop < HOPS:
            name = "collect_" + str(hop)
            near, total = collect(name, [up, down], [up_rows, down_rows], at, near_shape, share, near, total)

    rows_shape = (tile_counts.shape[0] * UROWS, features)
    near, copies, rows = finish([up, down], [up_rows, down_rows], at, near, total, replicas, rows_shape)
    other = core_swap(near, chips)
    gram = lax.all_to_all(copies.reshape(features, features), "rep", 0, 0, tiled=True)
    rows, started = first_residue(places, near, other, weight, item_factors, rows)
    return solve_steps(rows, weight, item_factors, started, gram)


def solution(mesh):
    in_specs = (
        P(("grp", "rep"), None),
        P(("grp", "rep"), None),
        P(("grp", "rep")),
        P(("grp", "rep"), None, None),
    )
    out_specs = P(("grp", "rep"), None)
    return jax.shard_map(
        on_device, mesh=mesh, in_specs=in_specs, out_specs=out_specs, check_vma=False
    )
```
